512 devices in a mesh: date: 16 (over z_hi, x, core), band: 32 (over z_lo, y).
Axes of the slice: x: 4, y: 4, z: 16 (z_hi: 2, z_lo: 8; z = z_hi * 8 + z_lo), core: 2. Of those that a mesh axis runs over, the one named last changes fastest.
Arguments:
- model_prognosis: bfloat16 [32, 2, 5, 128, 360], P('date', None, None, 'band'), may hold values from -6 to 6
- analysis_truth: bfloat16 [32, 2, 5, 512, 1440], P('date', None, None, 'band'), may hold values from -6 to 6
- expected_normal: bfloat16 [2, 5, 512, 1440], P(None, None, 'band'), may hold values from -5 to 5
- parallel_first_indices: int32 [512], P('band'), may hold values from -2 to 126, as said below
- parallel_blend_factors: float32 [512, 4], P('band'), may hold values from 0.05 to 0.5
- meridian_first_indices: int32 [1440], replicated, may hold values from 0 to 359, as said below
- meridian_blend_factors: bfloat16 [4, 1440], replicated, may hold values from 0.049804688 to 0.5
Outputs:
- sq_error: float32 [2, 5, 512, 1440], P(None, None, ('band', 'date'))
- anom_product: float32 [2, 5, 512, 1440], P(None, None, ('band', 'date'))
The draws below stay inside these ranges and needn't reach their ends.
Inputs may be any that keep to these rules, and one draw needn't show every extreme that they name: `parallel_first_indices`: fine row r's stencil starts at coarse row r // 4 - 2 or r // 4 - 1. `meridian_first_indices`: fine longitude x's stencil starts at coarse longitude (x // 4 - 1) or (x // 4), taken modulo 360.
All inputs are finite; a program needn't handle non-finite values.
Results may differ from the reference program's by a relative error of at most 0.0015.
Values may be sent and summed in bfloat16 or wider, within the bound.
A program may use at most 64 MiB of HBM per device.

```python
import jax
import jax.numpy as jnp
from jax import lax

ASSESSED_QUANTS = 5
OUTLOOK_OFFSETS = 2
SPARSE_EASTINGS = 360
DENSE_EASTINGS = 1440
SPARSE_NORTHINGS = 128
DENSE_NORTHINGS = 512
ISSUE_MOMENTS = 32


def stencil_start(key, count):
    positions = jnp.arange(count, dtype=jnp.int32)
    extra = jax.random.randint(key, (count,), 0, 2, dtype=jnp.int32)
    extra = jnp.where(positions % 4 == 0, 0, jnp.where(positions % 4 == 3, 1, extra))
    return positions // 4 + extra


def draw_parallel_first_indices(key, part):
    return stencil_start(jax.random.fold_in(key, 11), DENSE_NORTHINGS) - 2


def draw_meridian_first_indices(key, part):
    return (stencil_start(jax.random.fold_in(key, 23), DENSE_EASTINGS) - 1) % SPARSE_EASTINGS


def level_of(stream_key, extent, pieces, smallest, high):
    level = 1.0
    for dim, blocks in pieces:
        steps = jax.random.uniform(jax.random.fold_in(jax.random.fold_in(stream_key, 6), dim), (blocks,), jnp.float32, smallest / len(pieces), high / len(pieces))
        level = level * jnp.repeat(jnp.exp(steps), extent[dim] // blocks).reshape((-1,) + (1,) * (len(extent) - 1 - dim))
    return level


def bell_draw(key, extent, deviation, limit, cuts=(), held_as=jnp.bfloat16):
    entries = jax.random.normal(key, extent, jnp.float32) * deviation
    if len(cuts) > 0:
        entries = level_of(key, extent, cuts, -0.22, 0.18) * entries
    return jnp.clip(entries, min=-limit, max=limit).astype(held_as)


def setup_inputs(seed: int = 0) -> dict:
    splits = jax.random.split(jax.random.key(seed), 8)
    model_prognosis = bell_draw(splits[0], (ISSUE_MOMENTS, OUTLOOK_OFFSETS, ASSESSED_QUANTS, SPARSE_NORTHINGS, SPARSE_EASTINGS), 1.0, 6.0, ((0, 16), (3, 32)))
    analysis_truth = bell_draw(splits[1], (ISSUE_MOMENTS, OUTLOOK_OFFSETS, ASSESSED_QUANTS, DENSE_NORTHINGS, DENSE_EASTINGS), 1.0, 6.0, ((0, 16), (3, 32)))
    expected_normal = bell_draw(splits[2], (OUTLOOK_OFFSETS, ASSESSED_QUANTS, DENSE_NORTHINGS, DENSE_EASTINGS), 0.7, 5.0, ((2, 32),))
    parallel_first_indices = draw_parallel_first_indices(jax.random.fold_in(splits[7], 71), 0)
    parallel_blend_factors = jnp.clip(0.05 + 0.45 * jax.random.uniform(splits[4], (DENSE_NORTHINGS, 4), jnp.float32) ** level_of(splits[4], (DENSE_NORTHINGS, 4), ((0, 32),), -0.2, 0.2), 0.05, 0.5)
    meridian_first_indices = draw_meridian_first_indices(jax.random.fold_in(splits[7], 71), 0)
    meridian_blend_factors = jnp.clip(jax.random.uniform(splits[6], (4, DENSE_EASTINGS), jnp.float32, 0.049804688, 0.5), 0.049804688, 0.5).astype(jnp.bfloat16)
    return dict(model_prognosis=model_prognosis, analysis_truth=analysis_truth, expected_normal=expected_normal, parallel_first_indices=parallel_first_indices, parallel_blend_factors=parallel_blend_factors, meridian_first_indices=meridian_first_indices, meridian_blend_factors=meridian_blend_factors)


def reference(model_prognosis, analysis_truth, expected_normal, parallel_first_indices, parallel_blend_factors, meridian_first_indices, meridian_blend_factors):
    climate = expected_normal.astype(jnp.float32)
    weights_lon = meridian_blend_factors.astype(jnp.float32)

    def issue_instance(loop_accumulator, argument_bundle):
        fields, actual_bf = argument_bundle
        fields32 = fields.astype(jnp.float32)
        through_axis = jnp.zeros(fields.shape[:-1] + (DENSE_EASTINGS,), jnp.float32)
        for stencil in range(4):
            columns = ((meridian_first_indices + stencil) % SPARSE_EASTINGS).astype(jnp.int32)
            through_axis = through_axis + weights_lon[stencil] * jnp.take(fields32, columns, axis=3)
        widened_grid = jnp.pad(through_axis, ((0, 0), (0, 0), (2, 2), (0, 0)))
        fine = jnp.zeros(through_axis.shape[:2] + (DENSE_NORTHINGS, DENSE_EASTINGS), jnp.float32)
        for stencil in range(4):
            rows_index = (parallel_first_indices + 2 + stencil).astype(jnp.int32)
            fine = fine + parallel_blend_factors[:, stencil][:, None] * jnp.take(widened_grid, rows_index, axis=2)
        actual = actual_bf.astype(jnp.float32)
        error_map = fine - actual
        fcst_anom = fine - climate
        true_anom = actual - climate
        return (loop_accumulator[0] + error_map * error_map, loop_accumulator[1] + fcst_anom * true_anom), None

    blank_seed_arrays = jnp.zeros((OUTLOOK_OFFSETS, ASSESSED_QUANTS, DENSE_NORTHINGS, DENSE_EASTINGS), jnp.float32)
    prefix_additions, discarded_result = lax.scan(issue_instance, (blank_seed_arrays, blank_seed_arrays), (model_prognosis, analysis_truth))
    return prefix_additions[0] / ISSUE_MOMENTS, prefix_additions[1] / ISSUE_MOMENTS
```

```python
import functools

import jax
import jax.numpy as jnp
from jax import lax
from jax.experimental import pallas as pl
from jax.experimental.pallas import tpu as pltpu
from jax.sharding import PartitionSpec as P

MESH = pl.DeviceIdType.MESH
F32 = jnp.float32
BF16 = jnp.bfloat16
WIDE = 1440
COARSE = 360
CHUNK = 512
CHUNKS = 3


def kernel(
    model, truth, climate, starts, lat_w, lon_first, lon_w,
    out,
    tbuf, cbuf, crs, fields, table, pick, pick_c, xsend, xrecv, zsend, zown, zrecv,
    lsem, tsem, csend, crecv, xssem, xrsem, zssem, zrsem,
):
    date = lax.axis_index("date")
    band = lax.axis_index("band")
    bands = 32
    half = date // 8
    x = (date // 2) % 4
    core = date % 2

    def at(h, xx, c):
        return h * 8 + xx * 2 + c

    sibling = (at(half, x, 1 - core), band)
    across = [(at(half, (x + k) % 4, core), band) for k in (1, 2, 3)]
    far = (at(1 - half, x, core), band)
    up, down = (band + 1) % bands, (band + bands - 1) % bands
    near = [(date, up), (date, down), (at(half, x, 1 - core), up), (at(half, x, 1 - core), down)]
    barrier = pltpu.get_barrier_semaphore()
    for partner in [far, sibling] + near + across:
        pl.semaphore_signal(barrier, inc=1, device_id=partner, device_id_type=MESH)

    own_truth = pltpu.make_async_copy(truth, tbuf.at[0], lsem.at[0])
    own_truth.start()
    own_climate = pltpu.make_async_copy(climate, cbuf, lsem.at[1])
    own_climate.start()

    crs[0, 1:3] = jnp.zeros((2, 48, 384), BF16)
    m = model[...].astype(F32)
    for pair in range(2):
        rows = []
        for k in (2 * pair, 2 * pair + 1):
            plane = m[:, k, :]
            rows += [plane[0:8], plane[10:18]]
            a, b = plane[8:10], plane[18:20]
            rows += [a, a, b, b]
        crs[0, 1 + pair, :, 0:COARSE] = jnp.concatenate(rows, axis=0).astype(BF16)

    pl.semaphore_wait(barrier, 9)

    def send(src, dst, ssem, rsem, device):
        copy = pltpu.make_async_remote_copy(
            src_ref=src, dst_ref=dst, send_sem=ssem, recv_sem=rsem, device_id=device, device_id_type=MESH
        )
        copy.start()
        return copy

    coarse = [
        send(crs.at[0, 2], crs.at[0, 0], csend.at[0], crecv.at[0], near[0]),
        send(crs.at[0, 1], crs.at[0, 3], csend.at[1], crecv.at[1], near[1]),
        send(crs.at[0, 2], crs.at[1, 0], csend.at[2], crecv.at[2], near[2]),
        send(crs.at[0, 1], crs.at[1, 3], csend.at[3], crecv.at[3], near[3]),
        send(crs.at[0, pl.ds(1, 2)], crs.at[1, pl.ds(1, 2)], csend.at[4], crecv.at[4], sibling),
    ]
    other_truth = send(truth, tbuf.at[1], tsem.at[0], tsem.at[1], sibling)

    first_all = lon_first[...]
    weights_all = lon_w[...].astype(F32)
    for start in range(0, WIDE, CHUNK):
        width = min(CHUNK, WIDE - start)
        first = first_all[:, start : start + width]
        step = lax.broadcasted_iota(jnp.int32, (384, width), 0) - first
        step = jnp.where(step < 0, step + COARSE, step)
        block = jnp.zeros((384, width), F32)
        for k in range(4):
            block = jnp.where(step == k, weights_all[k : k + 1, start : start + width], block)
        row = lax.broadcasted_iota(jnp.int32, (384, width), 0)
        table[:, start : start + width] = jnp.where(row < COARSE, block, 0.0).astype(BF16)

    row = lax.broadcasted_iota(jnp.int32, (160, 1), 0)
    q = row - 128
    main = row < 128
    d_of = jnp.where(main, row // 64, (q % 8) // 4)
    x_of = jnp.where(main, (row % 64) // 16, q // 8)
    z_of = jnp.where(main, (row // 8) % 2, (q // 2) % 2)
    v_of = jnp.where(main, row % 8, 8 + q % 2)
    target = v_of * 16 + 8 * z_of + 2 * x_of + core
    column = lax.broadcasted_iota(jnp.int32, (160, 160), 1)
    pick_c[...] = (column == target).astype(F32).astype(BF16)
    column = lax.broadcasted_iota(jnp.int32, (160, 320), 1)
    pick[...] = (column == d_of * 160 + target).astype(F32).astype(BF16)
    xsend[:, CHUNKS - 1, :, 384:512] = jnp.zeros((4, 40, 128), F32)

    stencil = {}
    for xx in range(4):
        for z in range(2):
            r = 8 * z + 2 * xx + core
            base = 2 * z + xx // 2
            late = starts[r] - (4 * band + base - 2)
            w = [lat_w[k, r] for k in range(4)]
            five = [jnp.where(late == 0, w[0], 0.0)]
            five += [jnp.where(late == 0, w[j], w[j - 1]) for j in (1, 2, 3)]
            five += [jnp.where(late == 0, 0.0, w[3])]
            for j in range(5):
                value = five[j]
                if base + j < 2:
                    value = jnp.where(band == 0, 0.0, value)
                if base + j >= 6:
                    value = jnp.where(band == bands - 1, 0.0, value)
                stencil[xx, z, base + j] = value

    for copy in coarse:
        copy.wait_recv()
    zmask = (lax.broadcasted_iota(jnp.int32, (8, 384), 0) // 2) % 2 == 0
    for s in range(2):
        planes = []
        for pair in range(4):
            both = crs[s, pair].astype(F32)
            planes += [both[0:24], both[24:48]]

        def put(at_row, value):
            high = value.astype(BF16)
            low = (value - high.astype(F32)).astype(BF16)
            rows = value.shape[0]
            fields[0, s, at_row : at_row + rows, :] = high
            fields[1, s, at_row : at_row + rows, :] = low

        for d in range(2):
            for xx in range(4):
                pieces = []
                for z in range(2):
                    total = None
                    for j in range(5):
                        c = 2 * z + xx // 2 + j
                        term = stencil[xx, z, c] * planes[c][8 * d : 8 * d + 8]
                        total = term if total is None else total + term
                    pieces.append(total)
                put(d * 64 + xx * 16, jnp.concatenate(pieces, axis=0))
        for pairx in range(2):
            pieces = []
            for xx in (2 * pairx, 2 * pairx + 1):
                total = None
                for c in range(8):
                    w0, w1 = stencil.get((xx, 0, c)), stencil.get((xx, 1, c))
                    if w0 is None and w1 is None:
                        continue
                    w = jnp.where(zmask, 0.0 if w0 is None else w0, 0.0 if w1 is None else w1)
                    term = w * planes[c][16:24]
                    total = term if total is None else total + term
                pieces.append(total)
            put(128 + 16 * pairx, jnp.concatenate(pieces, axis=0))

    own_truth.wait()
    own_climate.wait()
    other_truth.wait_recv()
    xcopies = []
    for ch in range(CHUNKS):
        lo, hi = ch * CHUNK, min((ch + 1) * CHUNK, WIDE)
        width = hi - lo
        w = table[:, lo:hi]
        clim = jnp.dot(pick_c[...], cbuf[:, lo:hi], preferred_element_type=F32)
        sq = an = None
        for s in range(2):
            fine = jnp.dot(fields[0, s], w, preferred_element_type=F32)
            fine += jnp.dot(fields[1, s], w, preferred_element_type=F32)
            actual = jnp.dot(pick[...], tbuf[s, :, lo:hi], preferred_element_type=F32)
            error = fine - actual
            e2 = error * error
            ab = (fine - clim) * (actual - clim)
            sq = e2 if sq is None else sq + e2
            an = ab if an is None else an + ab
        upper = lax.broadcasted_iota(jnp.int32, (8, width), 0) < 4
        for xx in range(4):
            block = slice(16 * xx, 16 * xx + 16)
            block1 = slice(64 + 16 * xx, 64 + 16 * xx + 16)
            tail = slice(128 + 8 * xx, 136 + 8 * xx)
            xsend[xx, ch, 0:16, 0:width] = sq[block] + sq[block1]
            xsend[xx, ch, 16:32, 0:width] = an[block] + an[block1]
            mixed = []
            for t in (sq[tail], an[tail]):
                mixed.append(t + pltpu.roll(t, 4, 0))
            xsend[xx, ch, 32:40, 0:width] = jnp.where(upper, mixed[0], mixed[1])
        for k in range(3):
            xcopies.append(
                send(
                    xsend.at[(x + k + 1) % 4, ch],
                    xrecv.at[k, ch],
                    xssem.at[k, ch],
                    xrsem.at[k, ch],
                    across[k],
                )
            )

    first_half = half == 0
    even = lax.broadcasted_iota(jnp.int32, (8, 256), 0) % 4 < 2
    zcopies = []
    for ch in range(CHUNKS):
        total = xsend[x, ch]
        for k in range(3):
            xcopies[3 * ch + k].wait_recv()
            total += xrecv[k, ch]
        parts = []
        for z in range(2):
            a, b = total[8 * z : 8 * z + 8], total[16 + 8 * z : 24 + 8 * z]
            left, right = total[32:40, 0:256], total[32:40, 256:512]
            if z == 0:
                tail = jnp.where(even, left, pltpu.roll(right, 2, 0))
            else:
                tail = jnp.where(even, pltpu.roll(left, 6, 0), right)
            parts.append(
                jnp.concatenate([a[:, 0:256], b[:, 0:256], a[:, 256:512], b[:, 256:512], tail], axis=0)
            )
        zsend[ch] = jnp.where(first_half, parts[1], parts[0])
        zown[ch] = jnp.where(first_half, parts[0], parts[1])
        zcopies.append(send(zsend.at[ch], zrecv.at[ch], zssem.at[ch], zrsem.at[ch], far))

    for ch in range(CHUNKS):
        zcopies[ch].wait_recv()
        total = (zown[ch] + zrecv[ch]) * (1.0 / 32.0)
        for side in range(2):
            lo = ch * CHUNK + side * 256
            hi = min(lo + 256, WIDE)
            width = hi - lo
            for which in range(2):
                r = 16 * side + 8 * which
                out[which, 0:8, lo:hi] = total[r : r + 8, 0:width]
                r = 32 + 4 * which + 2 * side
                out[which, 8:10, lo:hi] = total[r : r + 2, 0:width]

    for copy in coarse + [other_truth] + xcopies + zcopies:
        copy.wait_send()


def shards(model, truth, climate, starts, lat_w, lon_first, lon_w):
    vmem = pl.BlockSpec(memory_space=pltpu.VMEM)
    smem = pl.BlockSpec(memory_space=pltpu.SMEM)
    hbm = pl.BlockSpec(memory_space=pl.ANY)
    maps = pl.pallas_call(
        kernel,
        out_shape=jax.ShapeDtypeStruct((2, 10, WIDE), F32),
        in_specs=[vmem, hbm, hbm, smem, smem, vmem, vmem],
        out_specs=vmem,
        scratch_shapes=[
            pltpu.VMEM((2, 320, WIDE), BF16),
            pltpu.VMEM((160, WIDE), BF16),
            pltpu.VMEM((2, 4, 48, 384), BF16),
            pltpu.VMEM((2, 2, 160, 384), BF16),
            pltpu.VMEM((384, WIDE), BF16),
            pltpu.VMEM((160, 320), BF16),
            pltpu.VMEM((160, 160), BF16),
            pltpu.VMEM((4, CHUNKS, 40, CHUNK), F32),
            pltpu.VMEM((3, CHUNKS, 40, CHUNK), F32),
            pltpu.VMEM((CHUNKS, 40, 256), F32),
            pltpu.VMEM((CHUNKS, 40, 256), F32),
            pltpu.VMEM((CHUNKS, 40, 256), F32),
            pltpu.SemaphoreType.DMA((2,)),
            pltpu.SemaphoreType.DMA((2,)),
            pltpu.SemaphoreType.DMA((5,)),
            pltpu.SemaphoreType.DMA((5,)),
            pltpu.SemaphoreType.DMA((3, CHUNKS)),
            pltpu.SemaphoreType.DMA((3, CHUNKS)),
            pltpu.SemaphoreType.DMA((CHUNKS,)),
            pltpu.SemaphoreType.DMA((CHUNKS,)),
        ],
        compiler_params=pltpu.CompilerParams(
            collective_id=0, has_side_effects=True, vmem_limit_bytes=40 * 2**20
        ),
    )(
        model.reshape(20, 4, COARSE),
        truth.reshape(320, WIDE),
        climate.reshape(160, WIDE),
        starts,
        lat_w.T,
        lon_first.reshape(1, WIDE),
        lon_w,
    )
    return maps[0].reshape(2, 5, 1, WIDE), maps[1].reshape(2, 5, 1, WIDE)


def solution(mesh):
    in_specs = (
        P("date", None, None, "band", None),
        P("date", None, None, "band", None),
        P(None, None, "band", None),
        P("band"),
        P("band", None),
        P(),
        P(),
    )
    out_specs = (P(None, None, ("band", "date"), None), P(None, None, ("band", "date"), None))
    return jax.shard_map(shards, mesh=mesh, in_specs=in_specs, out_specs=out_specs, check_vma=False)
```

```python
import functools

import jax
import jax.numpy as jnp
from jax import lax
from jax.experimental import pallas as pl
from jax.experimental.pallas import tpu as pltpu
from jax.sharding import PartitionSpec as P

MESH = pl.DeviceIdType.MESH
F32 = jnp.float32
BF16 = jnp.bfloat16
WIDE = 1440
COARSE = 360
CHUNK = 512
CHUNKS = 3


def upper_rows():
    return lax.broadcasted_iota(jnp.int32, (8, 128), 0) < 4


def encode(sqs, ans, tails):
    upper = upper_rows()

    def scale(tiles, keep):
        most = functools.reduce(jnp.maximum, [jnp.abs(t) for t in tiles])
        more = functools.reduce(jnp.maximum, [jnp.abs(t) for t in tails])
        most = jnp.maximum(jnp.maximum(most, jnp.where(keep, more, 0.0)), 1e-25)
        return jnp.ceil(jnp.log(most) * (8.0 / 0.6931471805599453) + 0.01)

    e_sq, e_an = scale(sqs, upper), scale(ans, jnp.logical_not(upper))
    up_sq, up_an = (32767.0 * jnp.exp2(e * -0.125) for e in (e_sq, e_an))
    up_tail = jnp.where(upper, up_sq, up_an)
    words = []
    for tiles, up in ((sqs, up_sq), (ans, up_an), (tails, up_tail)):
        codes = [jnp.round(t * up).astype(jnp.int32) for t in tiles]
        for low, high in zip(codes[0::2], codes[1::2], strict=True):
            words.append((high << 16) | (low & 0xFFFF))
    words.append((e_sq.astype(jnp.int32) << 16) | (e_an.astype(jnp.int32) & 0xFFFF))
    return jnp.concatenate(words, axis=0)


def decode(words, n, n_tail):
    count = words.shape[0] // 8
    tiles = [words[8 * i : 8 * i + 8] for i in range(count)]

    def both(t):
        return ((t << 16) >> 16).astype(F32), (t >> 16).astype(F32)

    e_an, e_sq = both(tiles[-1])
    down_sq, down_an = (jnp.exp2(e * 0.125) * (1.0 / 32767.0) for e in (e_sq, e_an))
    down_tail = jnp.where(upper_rows(), down_sq, down_an)
    values = []
    for i, t in enumerate(tiles[:-1]):
        down = down_sq if i < n // 2 else down_an if i < n else down_tail
        values += [v * down for v in both(t)]
    return values[:n], values[n : 2 * n], values[2 * n :]


def kernel(
    model, truth, climate, starts, lat_w, lon_first, lon_w,
    out,
    mbuf, tbuf, cbuf, crs, fields, table, pick, pick_c, parts, xsend, xrecv, zsend, zown, zrecv,
    lsem, tsem, csend, crecv, xssem, xrsem, zssem, zrsem, far_in,
):
    date = lax.axis_index("date")
    band = lax.axis_index("band")
    bands = 32
    half = date // 8
    x = (date // 2) % 4
    core = date % 2

    def at(h, xx, c):
        return h * 8 + xx * 2 + c

    sibling = (at(half, x, 1 - core), band)
    across = [(at(half, (x + k) % 4, core), band) for k in (1, 2, 3)]
    far = (at(1 - half, x, core), band)
    up, down = band + 1, band - 1
    near = [(date, up), (date, down), (at(half, x, 1 - core), up), (at(half, x, 1 - core), down)]
    not_last, not_first = band < bands - 1, band > 0
    barrier = pltpu.get_barrier_semaphore()

    def greet(partner):
        pl.semaphore_signal(barrier, inc=1, device_id=partner, device_id_type=MESH)

    pl.when(half == 0)(lambda: greet(far))
    pl.when(not_last)(lambda: [greet(near[0]), greet(near[2])] and None)
    pl.when(not_first)(lambda: [greet(near[1]), greet(near[3])] and None)
    for partner in [sibling] + across:
        greet(partner)

    own_model = pltpu.make_async_copy(model, mbuf, lsem.at[2])
    own_model.start()
    own_truth = pltpu.make_async_copy(truth, tbuf.at[0], lsem.at[0])
    own_truth.start()
    own_climate = pltpu.make_async_copy(climate, cbuf, lsem.at[1])
    own_climate.start()

    crs[0, 1:3] = jnp.zeros((2, 48, 384), BF16)
    own_model.wait()
    m = mbuf[...].astype(F32)
    for pair in range(2):
        rows = []
        for k in (2 * pair, 2 * pair + 1):
            plane = m[:, k, :]
            rows += [plane[0:8], plane[10:18]]
            a, b = plane[8:10], plane[18:20]
            rows += [a, a, b, b]
        crs[0, 1 + pair, :, 0:COARSE] = jnp.concatenate(rows, axis=0).astype(BF16)
    pl.semaphore_wait(
        barrier,
        4 + half + 2 * jnp.where(not_last, 1, 0) + 2 * jnp.where(not_first, 1, 0),
    )

    pending = []

    def make(src, dst, ssem, rsem, device):
        return pltpu.make_async_remote_copy(
            src_ref=src, dst_ref=dst, send_sem=ssem, recv_sem=rsem, device_id=device, device_id_type=MESH
        )

    def send(*what):
        copy = make(*what)
        copy.start()
        pending.append(copy)
        return copy

    edges = [
        make(crs.at[0, 2], crs.at[0, 0], csend.at[0], crecv.at[0], near[0]),
        make(crs.at[0, 1], crs.at[0, 3], csend.at[1], crecv.at[1], near[1]),
        make(crs.at[0, 2], crs.at[1, 0], csend.at[2], crecv.at[2], near[2]),
        make(crs.at[0, 1], crs.at[1, 3], csend.at[3], crecv.at[3], near[3]),
    ]

    @pl.when(not_last)
    def _():
        edges[0].start()
        edges[2].start()

    @pl.when(not_first)
    def _():
        edges[1].start()
        edges[3].start()

    swap = send(crs.at[0, pl.ds(1, 2)], crs.at[1, pl.ds(1, 2)], csend.at[4], crecv.at[4], sibling)

    @pl.when(half == 1)
    def _():
        pl.semaphore_signal(far_in, inc=1, device_id=far, device_id_type=MESH)

    other_truth = send(truth, tbuf.at[1], tsem.at[0], tsem.at[1], sibling)

    first_all = lon_first[...].reshape(1, WIDE)
    weights_all = lon_w[...].astype(F32)
    for start in range(0, WIDE, CHUNK):
        width = min(CHUNK, WIDE - start)
        first = first_all[:, start : start + width]
        step = lax.broadcasted_iota(jnp.int32, (384, width), 0) - first
        step = jnp.where(step < 0, step + COARSE, step)
        block = jnp.zeros((384, width), F32)
        for k in range(4):
            block = jnp.where(step == k, weights_all[k : k + 1, start : start + width], block)
        row = lax.broadcasted_iota(jnp.int32, (384, width), 0)
        table[:, start : start + width] = jnp.where(row < COARSE, block, 0.0).astype(BF16)

    row = lax.broadcasted_iota(jnp.int32, (160, 1), 0)
    q = row - 128
    main = row < 128
    d_of = jnp.where(main, row // 64, (q % 8) // 4)
    x_of = jnp.where(main, (row % 64) // 16, q // 8)
    z_of = jnp.where(main, (row // 8) % 2, (q // 2) % 2)
    v_of = jnp.where(main, row % 8, 8 + q % 2)
    target = v_of * 16 + 8 * z_of + 2 * x_of + core
    column = lax.broadcasted_iota(jnp.int32, (160, 160), 1)
    pick_c[...] = (column == target).astype(F32).astype(BF16)
    column = lax.broadcasted_iota(jnp.int32, (160, 320), 1)
    pick[...] = (column == d_of * 160 + target).astype(F32).astype(BF16)
    parts[:, CHUNKS - 1, :, 384:512] = jnp.zeros((4, 40, 128), F32)

    stencil = {}
    for xx in range(4):
        for z in range(2):
            r = 8 * z + 2 * xx + core
            base = 2 * z + xx // 2
            late = starts[r] - (4 * band + base - 2)
            w = [lat_w[k, r] for k in range(4)]
            five = [jnp.where(late == 0, w[0], 0.0)]
            five += [jnp.where(late == 0, w[j], w[j - 1]) for j in (1, 2, 3)]
            five += [jnp.where(late == 0, 0.0, w[3])]
            for j in range(5):
                stencil[xx, z, base + j] = five[j]

    @pl.when(not_first)
    def _():
        edges[0].wait_recv()
        edges[2].wait_recv()

    @pl.when(not_last)
    def _():
        edges[1].wait_recv()
        edges[3].wait_recv()

    @pl.when(band == 0)
    def _():
        crs[:, 0] = jnp.zeros((2, 48, 384), BF16)

    @pl.when(band == bands - 1)
    def _():
        crs[:, 3] = jnp.zeros((2, 48, 384), BF16)

    swap.wait_recv()
    zmask = (lax.broadcasted_iota(jnp.int32, (8, 384), 0) // 2) % 2 == 0
    for s in range(2):
        planes = []
        for pair in range(4):
            both = crs[s, pair].astype(F32)
            planes += [both[0:24], both[24:48]]

        def put(at_row, value):
            high = value.astype(BF16)
            low = (value - high.astype(F32)).astype(BF16)
            rows = value.shape[0]
            fields[0, s, at_row : at_row + rows, :] = high
            fields[1, s, at_row : at_row + rows, :] = low

        for d in range(2):
            for xx in range(4):
                pieces = []
                for z in range(2):
                    total = None
                    for j in range(5):
                        c = 2 * z + xx // 2 + j
                        term = stencil[xx, z, c] * planes[c][8 * d : 8 * d + 8]
                        total = term if total is None else total + term
                    pieces.append(total)
                put(d * 64 + xx * 16, jnp.concatenate(pieces, axis=0))
        for pairx in range(2):
            pieces = []
            for xx in (2 * pairx, 2 * pairx + 1):
                total = None
                for c in range(8):
                    w0, w1 = stencil.get((xx, 0, c)), stencil.get((xx, 1, c))
                    if w0 is None and w1 is None:
                        continue
                    w = jnp.where(zmask, 0.0 if w0 is None else w0, 0.0 if w1 is None else w1)
                    term = w * planes[c][16:24]
                    total = term if total is None else total + term
                pieces.append(total)
            put(128 + 16 * pairx, jnp.concatenate(pieces, axis=0))

    own_truth.wait()
    own_climate.wait()
    other_truth.wait_recv()
    xcopies = []
    for ch in range(CHUNKS):
        lo, hi = ch * CHUNK, min((ch + 1) * CHUNK, WIDE)
        width = hi - lo
        w = table[:, lo:hi]
        clim = jnp.dot(pick_c[...], cbuf[:, lo:hi], preferred_element_type=F32)
        sq = an = None
        for s in range(2):
            fine = jnp.dot(fields[0, s], w, preferred_element_type=F32)
            fine += jnp.dot(fields[1, s], w, preferred_element_type=F32)
            actual = jnp.dot(pick[...], tbuf[s, :, lo:hi], preferred_element_type=F32)
            error = fine - actual
            e2 = error * error
            ab = (fine - clim) * (actual - clim)
            sq = e2 if sq is None else sq + e2
            an = ab if an is None else an + ab
        upper = lax.broadcasted_iota(jnp.int32, (8, width), 0) < 4
        for xx in range(4):
            block = slice(16 * xx, 16 * xx + 16)
            block1 = slice(64 + 16 * xx, 64 + 16 * xx + 16)
            tail = slice(128 + 8 * xx, 136 + 8 * xx)
            parts[xx, ch, 0:16, 0:width] = sq[block] + sq[block1]
            parts[xx, ch, 16:32, 0:width] = an[block] + an[block1]
            mixed = []
            for t in (sq[tail], an[tail]):
                mixed.append(t + pltpu.roll(t, 4, 0))
            parts[xx, ch, 32:40, 0:width] = jnp.where(upper, mixed[0], mixed[1])
            block = parts[xx, ch]
            tiles = [block[:, 128 * j : 128 * j + 128] for j in range(4)]
            xsend[xx, ch] = encode(
                [t[r : r + 8] for r in (0, 8) for t in tiles],
                [t[r : r + 8] for r in (16, 24) for t in tiles],
                [t[32:40] for t in tiles],
            )
        for k in range(3):
            xcopies.append(
                send(
                    xsend.at[(x + k + 1) % 4, ch],
                    xrecv.at[k, ch],
                    xssem.at[k, ch],
                    xrsem.at[k, ch],
                    across[k],
                )
            )

    first_half = half == 0
    even = lax.broadcasted_iota(jnp.int32, (8, 256), 0) % 4 < 2
    zcopies = []
    for ch in range(CHUNKS):
        for k in range(3):
            xcopies[3 * ch + k].wait_recv()
        total = parts[x, ch]
        for k in range(3):
            sqs, ans, tails = decode(xrecv[k, ch], 8, 4)
            rows = [jnp.concatenate(g, axis=1) for g in (sqs[0:4], sqs[4:8], ans[0:4], ans[4:8], tails)]
            total += jnp.concatenate(rows, axis=0)
        kept = []
        for z in range(2):
            a, b = total[8 * z : 8 * z + 8], total[16 + 8 * z : 24 + 8 * z]
            left, right = total[32:40, 0:256], total[32:40, 256:512]
            if z == 0:
                tail = jnp.where(even, left, pltpu.roll(right, 2, 0))
            else:
                tail = jnp.where(even, pltpu.roll(left, 6, 0), right)
            kept.append(
                jnp.concatenate([a[:, 0:256], b[:, 0:256], a[:, 256:512], b[:, 256:512], tail], axis=0)
            )
        going = jnp.where(first_half, kept[1], kept[0])
        zown[ch] = jnp.where(first_half, kept[0], kept[1])
        tiles = [going[:, 128 * j : 128 * j + 128] for j in range(2)]
        zsend[ch] = encode(
            [t[r : r + 8] for r in (0, 16) for t in tiles],
            [t[r : r + 8] for r in (8, 24) for t in tiles],
            [t[32:40] for t in tiles],
        )
        if ch == 0:
            pl.when(first_half)(lambda: pl.semaphore_wait(far_in, 1))
        zcopies.append(send(zsend.at[ch], zrecv.at[ch], zssem.at[ch], zrsem.at[ch], far))

    for ch in range(CHUNKS):
        zcopies[ch].wait_recv()
        sqs, ans, tails = decode(zrecv[ch], 4, 2)
        rows = [jnp.concatenate(g, axis=1) for g in (sqs[0:2], ans[0:2], sqs[2:4], ans[2:4], tails)]
        total = (zown[ch] + jnp.concatenate(rows, axis=0)) * (1.0 / 32.0)
        for side in range(2):
            lo = ch * CHUNK + side * 256
            hi = min(lo + 256, WIDE)
            width = hi - lo
            for which in range(2):
                r = 16 * side + 8 * which
                out[which, 0:8, 0, lo:hi] = total[r : r + 8, 0:width]
                r = 32 + 4 * which + 2 * side
                out[which, 8:10, 0, lo:hi] = total[r : r + 2, 0:width]
    for copy in pending:
        copy.wait_send()

    @pl.when(not_last)
    def _():
        edges[0].wait_send()
        edges[2].wait_send()

    @pl.when(not_first)
    def _():
        edges[1].wait_send()
        edges[3].wait_send()


def shards(model, truth, climate, starts, lat_w, lon_first, lon_w):
    vmem = pl.BlockSpec(memory_space=pltpu.VMEM)
    smem = pl.BlockSpec(memory_space=pltpu.SMEM)
    hbm = pl.BlockSpec(memory_space=pl.ANY)
    maps = pl.pallas_call(
        kernel,
        out_shape=jax.ShapeDtypeStruct((2, 10, 1, WIDE), F32),
        in_specs=[hbm, hbm, hbm, smem, smem, vmem, vmem],
        out_specs=vmem,
        scratch_shapes=[
            pltpu.VMEM((20, 4, COARSE), BF16),
            pltpu.VMEM((2, 320, WIDE), BF16),
            pltpu.VMEM((160, WIDE), BF16),
            pltpu.VMEM((2, 4, 48, 384), BF16),
            pltpu.VMEM((2, 2, 160, 384), BF16),
            pltpu.VMEM((384, WIDE), BF16),
            pltpu.VMEM((160, 320), BF16),
            pltpu.VMEM((160, 160), BF16),
            pltpu.VMEM((4, CHUNKS, 40, CHUNK), F32),
            pltpu.VMEM((4, CHUNKS, 88, 128), jnp.int32),
            pltpu.VMEM((3, CHUNKS, 88, 128), jnp.int32),
            pltpu.VMEM((CHUNKS, 48, 128), jnp.int32),
            pltpu.VMEM((CHUNKS, 40, 256), F32),
            pltpu.VMEM((CHUNKS, 48, 128), jnp.int32),
            pltpu.SemaphoreType.DMA((3,)),
            pltpu.SemaphoreType.DMA((2,)),
            pltpu.SemaphoreType.DMA((5,)),
            pltpu.SemaphoreType.DMA((5,)),
            pltpu.SemaphoreType.DMA((3, CHUNKS)),
            pltpu.SemaphoreType.DMA((3, CHUNKS)),
            pltpu.SemaphoreType.DMA((CHUNKS,)),
            pltpu.SemaphoreType.DMA((CHUNKS,)),
            pltpu.SemaphoreType.REGULAR,
        ],
        compiler_params=pltpu.CompilerParams(
            collective_id=0, has_side_effects=True, vmem_limit_bytes=60 * 2**20
        ),
    )(
        model.reshape(20, 4, COARSE),
        truth.reshape(320, WIDE),
        climate.reshape(160, WIDE),
        starts,
        lat_w.T,
        lon_first,
        lon_w,
    )
    return maps[0].reshape(2, 5, 1, WIDE), maps[1].reshape(2, 5, 1, WIDE)


def solution(mesh):
    in_specs = (
        P("date", None, None, "band", None),
        P("date", None, None, "band", None),
        P(None, None, "band", None),
        P("band"),
        P("band", None),
        P(),
        P(),
    )
    out_specs = (P(None, None, ("band", "date"), None), P(None, None, ("band", "date"), None))
    return jax.shard_map(shards, mesh=mesh, in_specs=in_specs, out_specs=out_specs, check_vma=False)
```

```python
import functools

import jax
import jax.numpy as jnp
from jax import lax
from jax.experimental import pallas as pl
from jax.experimental.pallas import tpu as pltpu
from jax.sharding import PartitionSpec as P

MESH = pl.DeviceIdType.MESH
F32 = jnp.float32
BF16 = jnp.bfloat16
WIDE = 1440
COARSE = 360
CHUNK = 512
CHUNKS = 3


def upper_rows():
    return lax.broadcasted_iota(jnp.int32, (8, 128), 0) < 4


def encode(sqs, ans, tails):
    upper = upper_rows()

    def scale(tiles, keep):
        most = functools.reduce(jnp.maximum, [jnp.abs(t) for t in tiles])
        more = functools.reduce(jnp.maximum, [jnp.abs(t) for t in tails])
        most = jnp.maximum(jnp.maximum(most, jnp.where(keep, more, 0.0)), 1e-25)
        return jnp.ceil(jnp.log(most) * (8.0 / 0.6931471805599453) + 0.01)

    e_sq, e_an = scale(sqs, upper), scale(ans, jnp.logical_not(upper))
    up_sq, up_an = (32767.0 * jnp.exp2(e * -0.125) for e in (e_sq, e_an))
    up_tail = jnp.where(upper, up_sq, up_an)
    words = []
    for tiles, up in ((sqs, up_sq), (ans, up_an), (tails, up_tail)):
        codes = [jnp.round(t * up).astype(jnp.int32) for t in tiles]
        for low, high in zip(codes[0::2], codes[1::2], strict=True):
            words.append((high << 16) | (low & 0xFFFF))
    words.append((e_sq.astype(jnp.int32) << 16) | (e_an.astype(jnp.int32) & 0xFFFF))
    return jnp.concatenate(words, axis=0)


def decode(words, n, n_tail):
    count = words.shape[0] // 8
    tiles = [words[8 * i : 8 * i + 8] for i in range(count)]

    def both(t):
        return ((t << 16) >> 16).astype(F32), (t >> 16).astype(F32)

    e_an, e_sq = both(tiles[-1])
    down_sq, down_an = (jnp.exp2(e * 0.125) * (1.0 / 32767.0) for e in (e_sq, e_an))
    down_tail = jnp.where(upper_rows(), down_sq, down_an)
    values = []
    for i, t in enumerate(tiles[:-1]):
        down = down_sq if i < n // 2 else down_an if i < n else down_tail
        values += [v * down for v in both(t)]
    return values[:n], values[n : 2 * n], values[2 * n :]


def kernel(
    model, truth, climate, starts_in, lat_w_in, lon_first_in, lon_w_in,
    out,
    starts, lat_w, lon_first, lon_w, mbuf, tbuf, cbuf, crs, fields, table, pick, pick_c, actual, anomaly, mixed, parts, xsend, xrecv, zsend, zown, zrecv,
    lsem, tsem, csend, crecv, xssem, xrsem, zssem, zrsem, far_in,
):
    date = lax.axis_index("date")
    band = lax.axis_index("band")
    bands = 32
    half = date // 8
    x = (date // 2) % 4
    core = date % 2

    def at(h, xx, c):
        return h * 8 + xx * 2 + c

    sibling = (at(half, x, 1 - core), band)
    across = [(at(half, (x + k) % 4, core), band) for k in (1, 2, 3)]
    far = (at(1 - half, x, core), band)
    up, down = band + 1, band - 1
    near = [(date, up), (date, down), (at(half, x, 1 - core), up), (at(half, x, 1 - core), down)]
    not_last, not_first = band < bands - 1, band > 0
    barrier = pltpu.get_barrier_semaphore()

    def greet(partner):
        pl.semaphore_signal(barrier, inc=1, device_id=partner, device_id_type=MESH)

    pl.when(half == 0)(lambda: greet(far))
    pl.when(not_last)(lambda: [greet(near[0]), greet(near[2])] and None)
    pl.when(not_first)(lambda: [greet(near[1]), greet(near[3])] and None)
    for partner in [sibling] + across:
        greet(partner)

    own_model = pltpu.make_async_copy(model, mbuf, lsem.at[2])
    own_model.start()
    own_truth = pltpu.make_async_copy(truth, tbuf.at[0], lsem.at[0])
    own_truth.start()
    own_climate = pltpu.make_async_copy(climate, cbuf, lsem.at[1])
    own_climate.start()
    small = [
        pltpu.make_async_copy(source, target, lsem.at[3 + i])
        for i, (source, target) in enumerate(
            [(starts_in, starts), (lat_w_in, lat_w), (lon_first_in, lon_first), (lon_w_in, lon_w)]
        )
    ]
    for copy in small:
        copy.start()

    crs[0, 1:3] = jnp.zeros((2, 48, 384), BF16)
    own_model.wait()
    m = mbuf[...].astype(F32)
    for pair in range(2):
        rows = []
        for k in (2 * pair, 2 * pair + 1):
            plane = m[:, k, :]
            rows += [plane[0:8], plane[10:18]]
            a, b = plane[8:10], plane[18:20]
            rows += [a, a, b, b]
        crs[0, 1 + pair, :, 0:COARSE] = jnp.concatenate(rows, axis=0).astype(BF16)
    pl.semaphore_wait(
        barrier,
        4 + half + 2 * jnp.where(not_last, 1, 0) + 2 * jnp.where(not_first, 1, 0),
    )

    pending = []

    def make(src, dst, ssem, rsem, device):
        return pltpu.make_async_remote_copy(
            src_ref=src, dst_ref=dst, send_sem=ssem, recv_sem=rsem, device_id=device, device_id_type=MESH
        )

    def send(*what):
        copy = make(*what)
        copy.start()
        pending.append(copy)
        return copy

    edges = [
        make(crs.at[0, 2], crs.at[0, 0], csend.at[0], crecv.at[0], near[0]),
        make(crs.at[0, 1], crs.at[0, 3], csend.at[1], crecv.at[1], near[1]),
        make(crs.at[0, 2], crs.at[1, 0], csend.at[2], crecv.at[2], near[2]),
        make(crs.at[0, 1], crs.at[1, 3], csend.at[3], crecv.at[3], near[3]),
    ]

    @pl.when(not_last)
    def _():
        edges[0].start()
        edges[2].start()

    @pl.when(not_first)
    def _():
        edges[1].start()
        edges[3].start()

    swap = send(crs.at[0, pl.ds(1, 2)], crs.at[1, pl.ds(1, 2)], csend.at[4], crecv.at[4], sibling)

    @pl.when(half == 1)
    def _():
        pl.semaphore_signal(far_in, inc=1, device_id=far, device_id_type=MESH)

    other_truth = send(truth, tbuf.at[1], tsem.at[0], tsem.at[1], sibling)

    for copy in small:
        copy.wait()
    first_all = lon_first[...].reshape(1, WIDE)
    weights_all = lon_w[...].astype(F32)
    for start in range(0, WIDE, CHUNK):
        width = min(CHUNK, WIDE - start)
        first = first_all[:, start : start + width]
        step = lax.broadcasted_iota(jnp.int32, (384, width), 0) - first
        step = jnp.where(step < 0, step + COARSE, step)
        block = jnp.zeros((384, width), F32)
        for k in range(4):
            block = jnp.where(step == k, weights_all[k : k + 1, start : start + width], block)
        row = lax.broadcasted_iota(jnp.int32, (384, width), 0)
        table[:, start : start + width] = jnp.where(row < COARSE, block, 0.0).astype(BF16)

    row = lax.broadcasted_iota(jnp.int32, (160, 1), 0)
    q = row - 128
    main = row < 128
    d_of = jnp.where(main, row // 64, (q % 8) // 4)
    x_of = jnp.where(main, (row % 64) // 16, q // 8)
    z_of = jnp.where(main, (row // 8) % 2, (q // 2) % 2)
    v_of = jnp.where(main, row % 8, 8 + q % 2)
    target = v_of * 16 + 8 * z_of + 2 * x_of + core
    column = lax.broadcasted_iota(jnp.int32, (160, 160), 1)
    pick_c[...] = (column == target).astype(F32).astype(BF16)
    column = lax.broadcasted_iota(jnp.int32, (160, 320), 1)
    pick[...] = (column == d_of * 160 + target).astype(F32).astype(BF16)
    mixed[CHUNKS - 1, :, :, 384:512] = jnp.zeros((4, 8, 128), F32)
    parts[:, :, CHUNKS - 1, 16:32, 128:256] = jnp.zeros((4, 2, 16, 128), F32)

    stencil = {}
    for xx in range(4):
        for z in range(2):
            r = 8 * z + 2 * xx + core
            base = 2 * z + xx // 2
            late = starts[r] - (4 * band + base - 2)
            w = [lat_w[k, r] for k in range(4)]
            five = [jnp.where(late == 0, w[0], 0.0)]
            five += [jnp.where(late == 0, w[j], w[j - 1]) for j in (1, 2, 3)]
            five += [jnp.where(late == 0, 0.0, w[3])]
            for j in range(5):
                stencil[xx, z, base + j] = five[j]

    spans = [(lo, min(lo + CHUNK, WIDE)) for lo in range(0, WIDE, CHUNK)]
    own_climate.wait()
    own_truth.wait()
    for s in range(2):
        if s == 1:
            other_truth.wait_recv()
        for lo, hi in spans:
            t = jnp.dot(pick[...], tbuf[s, :, lo:hi], preferred_element_type=F32)
            clim = jnp.dot(pick_c[...], cbuf[:, lo:hi], preferred_element_type=F32)
            actual[s, :, lo:hi] = t
            anomaly[s, :, lo:hi] = t - clim

    @pl.when(not_first)
    def _():
        edges[0].wait_recv()
        edges[2].wait_recv()

    @pl.when(not_last)
    def _():
        edges[1].wait_recv()
        edges[3].wait_recv()

    @pl.when(band == 0)
    def _():
        crs[:, 0] = jnp.zeros((2, 48, 384), BF16)

    @pl.when(band == bands - 1)
    def _():
        crs[:, 3] = jnp.zeros((2, 48, 384), BF16)

    swap.wait_recv()
    zmask = (lax.broadcasted_iota(jnp.int32, (8, 384), 0) // 2) % 2 == 0
    for s in range(2):
        planes = []
        for pair in range(4):
            both = crs[s, pair].astype(F32)
            planes += [both[0:24], both[24:48]]

        def put(at_row, value):
            high = value.astype(BF16)
            low = (value - high.astype(F32)).astype(BF16)
            rows = value.shape[0]
            fields[0, s, at_row : at_row + rows, :] = high
            fields[1, s, at_row : at_row + rows, :] = low

        for d in range(2):
            for xx in range(4):
                pieces = []
                for z in range(2):
                    total = None
                    for j in range(5):
                        c = 2 * z + xx // 2 + j
                        term = stencil[xx, z, c] * planes[c][8 * d : 8 * d + 8]
                        total = term if total is None else total + term
                    pieces.append(total)
                put(d * 64 + xx * 16, jnp.concatenate(pieces, axis=0))
        for pairx in range(2):
            pieces = []
            for xx in (2 * pairx, 2 * pairx + 1):
                total = None
                for c in range(8):
                    w0, w1 = stencil.get((xx, 0, c)), stencil.get((xx, 1, c))
                    if w0 is None and w1 is None:
                        continue
                    w = jnp.where(zmask, 0.0 if w0 is None else w0, 0.0 if w1 is None else w1)
                    term = w * planes[c][16:24]
                    total = term if total is None else total + term
                pieces.append(total)
            put(128 + 16 * pairx, jnp.concatenate(pieces, axis=0))

    going, staying = 1 - half, half
    even = lax.broadcasted_iota(jnp.int32, (8, 256), 0) % 4 < 2

    def coded(block):
        tiles = [block[:, 0:128], block[:, 128:256]]
        return encode(
            [t[r : r + 8] for r in (0, 16) for t in tiles],
            [t[r : r + 8] for r in (8, 24) for t in tiles],
            [t[32:40] for t in tiles],
        )

    def plain(words):
        sqs, ans, tails = decode(words, 4, 2)
        rows = [jnp.concatenate(g, axis=1) for g in (sqs[0:2], ans[0:2], sqs[2:4], ans[2:4], tails)]
        return jnp.concatenate(rows, axis=0)

    def hand_over(which, rows, ch):
        copies = []
        for k in range(3):
            xsend[k, which, ch] = coded(parts[(x + k + 1) % 4, rows, ch])
            copies.append(
                send(
                    xsend.at[k, which, ch],
                    xrecv.at[k, which, ch],
                    xssem.at[k, which, ch],
                    xrsem.at[k, which, ch],
                    across[k],
                )
            )
        return copies

    def collect(which, rows, ch, copies):
        total = parts[x, rows, ch]
        for k in range(3):
            copies[k].wait_recv()
            total += plain(xrecv[k, which, ch])
        return total

    first, second = [], []
    for ch, (lo, hi) in enumerate(spans):
        width = hi - lo
        w = table[:, lo:hi]
        sq = an = None
        for s in range(2):
            fine = jnp.dot(fields[0, s], w, preferred_element_type=F32)
            fine += jnp.dot(fields[1, s], w, preferred_element_type=F32)
            error = fine - actual[s, :, lo:hi]
            true_anomaly = anomaly[s, :, lo:hi]
            e2 = error * error
            ab = (error + true_anomaly) * true_anomaly
            sq = e2 if sq is None else sq + e2
            an = ab if an is None else an + ab
        upper = lax.broadcasted_iota(jnp.int32, (8, width), 0) < 4
        for xx in range(4):
            tail = slice(128 + 8 * xx, 136 + 8 * xx)
            both = [t + pltpu.roll(t, 4, 0) for t in (sq[tail], an[tail])]
            mixed[ch, xx, :, 0:width] = jnp.where(upper, both[0], both[1])
            left, right = mixed[ch, xx, :, 0:256], mixed[ch, xx, :, 256:512]
            parts[xx, 0, ch, 32:40] = jnp.where(even, left, pltpu.roll(right, 2, 0))
            parts[xx, 1, ch, 32:40] = jnp.where(even, pltpu.roll(left, 6, 0), right)
            for z in range(2):
                r = 16 * xx + 8 * z
                for i, t in enumerate((sq, an)):
                    value = t[r : r + 8] + t[64 + r : 72 + r]
                    parts[xx, z, ch, 8 * i : 8 * i + 8] = value[:, 0:256]
                    parts[xx, z, ch, 16 + 8 * i : 24 + 8 * i, 0 : width - 256] = value[:, 256:width]
        first.append(hand_over(0, going, ch))
    for ch in range(CHUNKS):
        second.append(hand_over(1, staying, ch))

    zcopies = []
    for ch in range(CHUNKS):
        zsend[ch] = coded(collect(0, going, ch, first[ch]))
        if ch == 0:
            pl.when(half == 0)(lambda: pl.semaphore_wait(far_in, 1))
        zcopies.append(send(zsend.at[ch], zrecv.at[ch], zssem.at[ch], zrsem.at[ch], far))

    for ch in range(CHUNKS):
        zown[ch] = collect(1, staying, ch, second[ch])

    for ch, (start, _) in enumerate(spans):
        zcopies[ch].wait_recv()
        total = (zown[ch] + plain(zrecv[ch])) * (1.0 / 32.0)
        for side in range(2):
            lo = start + side * 256
            hi = min(lo + 256, WIDE)
            width = hi - lo
            for which in range(2):
                r = 16 * side + 8 * which
                out[which, 0:8, 0, lo:hi] = total[r : r + 8, 0:width]
                r = 32 + 4 * which + 2 * side
                out[which, 8:10, 0, lo:hi] = total[r : r + 2, 0:width]

    for copy in pending:
        copy.wait_send()

    @pl.when(not_last)
    def _():
        edges[0].wait_send()
        edges[2].wait_send()

    @pl.when(not_first)
    def _():
        edges[1].wait_send()
        edges[3].wait_send()


def shards(model, truth, climate, starts, lat_w, lon_first, lon_w):
    vmem = pl.BlockSpec(memory_space=pltpu.VMEM)
    hbm = pl.BlockSpec(memory_space=pl.ANY)
    maps = pl.pallas_call(
        kernel,
        out_shape=jax.ShapeDtypeStruct((2, 10, 1, WIDE), F32),
        in_specs=[hbm] * 7,
        out_specs=vmem,
        scratch_shapes=[
            pltpu.SMEM((16,), jnp.int32),
            pltpu.SMEM((4, 16), F32),
            pltpu.VMEM((WIDE,), jnp.int32),
            pltpu.VMEM((4, WIDE), BF16),
            pltpu.VMEM((20, 4, COARSE), BF16),
            pltpu.VMEM((2, 320, WIDE), BF16),
            pltpu.VMEM((160, WIDE), BF16),
            pltpu.VMEM((2, 4, 48, 384), BF16),
            pltpu.VMEM((2, 2, 160, 384), BF16),
            pltpu.VMEM((384, WIDE), BF16),
            pltpu.VMEM((160, 320), BF16),
            pltpu.VMEM((160, 160), BF16),
            pltpu.VMEM((2, 160, WIDE), F32),
            pltpu.VMEM((2, 160, WIDE), F32),
            pltpu.VMEM((CHUNKS, 4, 8, CHUNK), F32),
            pltpu.VMEM((4, 2, CHUNKS, 40, 256), F32),
            pltpu.VMEM((3, 2, CHUNKS, 48, 128), jnp.int32),
            pltpu.VMEM((3, 2, CHUNKS, 48, 128), jnp.int32),
            pltpu.VMEM((CHUNKS, 48, 128), jnp.int32),
            pltpu.VMEM((CHUNKS, 40, 256), F32),
            pltpu.VMEM((CHUNKS, 48, 128), jnp.int32),
            pltpu.SemaphoreType.DMA((7,)),
            pltpu.SemaphoreType.DMA((2,)),
            pltpu.SemaphoreType.DMA((5,)),
            pltpu.SemaphoreType.DMA((5,)),
            pltpu.SemaphoreType.DMA((3, 2, CHUNKS)),
            pltpu.SemaphoreType.DMA((3, 2, CHUNKS)),
            pltpu.SemaphoreType.DMA((CHUNKS,)),
            pltpu.SemaphoreType.DMA((CHUNKS,)),
            pltpu.SemaphoreType.REGULAR,
        ],
        compiler_params=pltpu.CompilerParams(
            collective_id=0, has_side_effects=True, vmem_limit_bytes=48 * 2**20
        ),
    )(
        *(
            pltpu.with_memory_space_constraint(operand, pltpu.HBM)
            for operand in (
                model.reshape(20, 4, COARSE),
                truth.reshape(320, WIDE),
                climate.reshape(160, WIDE),
                starts,
                lat_w.T,
                lon_first,
                lon_w,
            )
        )
    )
    return maps[0].reshape(2, 5, 1, WIDE), maps[1].reshape(2, 5, 1, WIDE)


def solution(mesh):
    in_specs = (
        P("date", None, None, "band", None),
        P("date", None, None, "band", None),
        P(None, None, "band", None),
        P("band"),
        P("band", None),
        P(),
        P(),
    )
    out_specs = (P(None, None, ("band", "date"), None), P(None, None, ("band", "date"), None))
    return jax.shard_map(shards, mesh=mesh, in_specs=in_specs, out_specs=out_specs, check_vma=False)
```

```python
import functools

import jax
import jax.numpy as jnp
from jax import lax
from jax.experimental import pallas as pl
from jax.experimental.pallas import tpu as pltpu
from jax.sharding import PartitionSpec as P

MESH = pl.DeviceIdType.MESH
F32 = jnp.float32
BF16 = jnp.bfloat16
WIDE = 1440
COARSE = 360
CHUNK = 512
CHUNKS = 3


def upper_rows():
    return lax.broadcasted_iota(jnp.int32, (8, 128), 0) < 4


def encode(sqs, ans, tails):
    upper = upper_rows()

    def scale(tiles, keep):
        most = functools.reduce(jnp.maximum, [jnp.abs(t) for t in tiles])
        more = functools.reduce(jnp.maximum, [jnp.abs(t) for t in tails])
        most = jnp.maximum(jnp.maximum(most, jnp.where(keep, more, 0.0)), 1e-25)
        return jnp.ceil(jnp.log(most) * (8.0 / 0.6931471805599453) + 0.01)

    e_sq, e_an = scale(sqs, upper), scale(ans, jnp.logical_not(upper))
    up_sq, up_an = (32767.0 * jnp.exp2(e * -0.125) for e in (e_sq, e_an))
    up_tail = jnp.where(upper, up_sq, up_an)
    words = []
    for tiles, up in ((sqs, up_sq), (ans, up_an), (tails, up_tail)):
        codes = [jnp.round(t * up).astype(jnp.int32) for t in tiles]
        for low, high in zip(codes[0::2], codes[1::2], strict=True):
            words.append((high << 16) | (low & 0xFFFF))
    words.append((e_sq.astype(jnp.int32) << 16) | (e_an.astype(jnp.int32) & 0xFFFF))
    return jnp.concatenate(words, axis=0)


def decode(words, n, n_tail):
    count = words.shape[0] // 8
    tiles = [words[8 * i : 8 * i + 8] for i in range(count)]

    def both(t):
        return ((t << 16) >> 16).astype(F32), (t >> 16).astype(F32)

    e_an, e_sq = both(tiles[-1])
    down_sq, down_an = (jnp.exp2(e * 0.125) * (1.0 / 32767.0) for e in (e_sq, e_an))
    down_tail = jnp.where(upper_rows(), down_sq, down_an)
    values = []
    for i, t in enumerate(tiles[:-1]):
        down = down_sq if i < n // 2 else down_an if i < n else down_tail
        values += [v * down for v in both(t)]
    return values[:n], values[n : 2 * n], values[2 * n :]


def kernel(
    model, truth, climate, starts_in, lat_w_in, lon_first_in, lon_w_in,
    out,
    starts, lat_w, lon_first, lon_w, mbuf, tbuf, cbuf, crs, fields, table, pick, pick_c, actual, anomaly, mixed, parts, xsend, xrecv, zsend, zown, zrecv,
    lsem, tsem, csend, crecv, xssem, xrsem, zssem, zrsem, far_in,
):
    date = lax.axis_index("date")
    band = lax.axis_index("band")
    bands = 32
    half = date // 8
    x = (date // 2) % 4
    core = date % 2

    def at(h, xx, c):
        return h * 8 + xx * 2 + c

    sibling = (at(half, x, 1 - core), band)
    across = [(at(half, (x + k) % 4, core), band) for k in (1, 2, 3)]
    far = (at(1 - half, x, core), band)
    up, down = band + 1, band - 1
    near = [(date, up), (date, down), (at(half, x, 1 - core), up), (at(half, x, 1 - core), down)]
    not_last, not_first = band < bands - 1, band > 0
    barrier = pltpu.get_barrier_semaphore()

    def greet(partner):
        pl.semaphore_signal(barrier, inc=1, device_id=partner, device_id_type=MESH)

    pl.when(half == 0)(lambda: greet(far))
    pl.when(not_last)(lambda: [greet(near[0]), greet(near[2])] and None)
    pl.when(not_first)(lambda: [greet(near[1]), greet(near[3])] and None)
    for partner in [sibling] + across:
        greet(partner)

    own_model = pltpu.make_async_copy(model, mbuf, lsem.at[2])
    own_model.start()
    own_truth = pltpu.make_async_copy(truth, tbuf.at[0], lsem.at[0])
    own_truth.start()
    own_climate = pltpu.make_async_copy(climate, cbuf, lsem.at[1])
    own_climate.start()
    small = [
        pltpu.make_async_copy(source, target, lsem.at[3 + i])
        for i, (source, target) in enumerate(
            [(starts_in, starts), (lat_w_in, lat_w), (lon_first_in, lon_first), (lon_w_in, lon_w)]
        )
    ]
    for copy in small:
        copy.start()

    crs[0, 1:3] = jnp.zeros((2, 48, 384), BF16)
    own_model.wait()
    m = mbuf[...].astype(F32)
    for pair in range(2):
        rows = []
        for k in (2 * pair, 2 * pair + 1):
            plane = m[:, k, :]
            rows += [plane[0:8], plane[10:18]]
            a, b = plane[8:10], plane[18:20]
            rows += [a, a, b, b]
        crs[0, 1 + pair, :, 0:COARSE] = jnp.concatenate(rows, axis=0).astype(BF16)
    pl.semaphore_wait(
        barrier,
        4 + half + 2 * jnp.where(not_last, 1, 0) + 2 * jnp.where(not_first, 1, 0),
    )

    pending = []

    def make(src, dst, ssem, rsem, device):
        return pltpu.make_async_remote_copy(
            src_ref=src, dst_ref=dst, send_sem=ssem, recv_sem=rsem, device_id=device, device_id_type=MESH
        )

    def send(*what):
        copy = make(*what)
        copy.start()
        pending.append(copy)
        return copy

    edges = [
        make(crs.at[0, 2], crs.at[0, 0], csend.at[0], crecv.at[0], near[0]),
        make(crs.at[0, 1], crs.at[0, 3], csend.at[1], crecv.at[1], near[1]),
        make(crs.at[0, 2], crs.at[1, 0], csend.at[2], crecv.at[2], near[2]),
        make(crs.at[0, 1], crs.at[1, 3], csend.at[3], crecv.at[3], near[3]),
    ]

    @pl.when(not_last)
    def _():
        edges[0].start()
        edges[2].start()

    @pl.when(not_first)
    def _():
        edges[1].start()
        edges[3].start()

    swap = send(crs.at[0, pl.ds(1, 2)], crs.at[1, pl.ds(1, 2)], csend.at[4], crecv.at[4], sibling)

    @pl.when(half == 1)
    def _():
        pl.semaphore_signal(far_in, inc=1, device_id=far, device_id_type=MESH)

    other_truth = send(truth, tbuf.at[1], tsem.at[0], tsem.at[1], sibling)

    for copy in small:
        copy.wait()
    first_all = lon_first[...].reshape(1, WIDE)
    weights_all = lon_w[...].astype(F32)
    for start in range(0, WIDE, CHUNK):
        width = min(CHUNK, WIDE - start)
        first = first_all[:, start : start + width]
        step = lax.broadcasted_iota(jnp.int32, (384, width), 0) - first
        step = jnp.where(step < 0, step + COARSE, step)
        block = jnp.zeros((384, width), F32)
        for k in range(4):
            block = jnp.where(step == k, weights_all[k : k + 1, start : start + width], block)
        row = lax.broadcasted_iota(jnp.int32, (384, width), 0)
        table[:, start : start + width] = jnp.where(row < COARSE, block, 0.0).astype(BF16)

    row = lax.broadcasted_iota(jnp.int32, (160, 1), 0)
    q = row - 128
    main = row < 128
    d_of = jnp.where(main, row // 64, (q % 8) // 4)
    x_of = jnp.where(main, (row % 64) // 16, q // 8)
    z_of = jnp.where(main, (row // 8) % 2, (q // 2) % 2)
    v_of = jnp.where(main, row % 8, 8 + q % 2)
    target = v_of * 16 + 8 * z_of + 2 * x_of + core
    column = lax.broadcasted_iota(jnp.int32, (160, 160), 1)
    pick_c[...] = (column == target).astype(F32).astype(BF16)
    column = lax.broadcasted_iota(jnp.int32, (160, 320), 1)
    pick[...] = (column == d_of * 160 + target).astype(F32).astype(BF16)
    mixed[CHUNKS - 1, :, :, 384:512] = jnp.zeros((4, 8, 128), F32)
    parts[:, :, CHUNKS - 1, 16:32, 128:256] = jnp.zeros((4, 2, 16, 128), F32)

    stencil = {}
    for xx in range(4):
        for z in range(2):
            r = 8 * z + 2 * xx + core
            base = 2 * z + xx // 2
            late = starts[r] - (4 * band + base - 2)
            w = [lat_w[k, r] for k in range(4)]
            five = [jnp.where(late == 0, w[0], 0.0)]
            five += [jnp.where(late == 0, w[j], w[j - 1]) for j in (1, 2, 3)]
            five += [jnp.where(late == 0, 0.0, w[3])]
            for j in range(5):
                stencil[xx, z, base + j] = five[j]

    spans = [(lo, min(lo + CHUNK, WIDE)) for lo in range(0, WIDE, CHUNK)]
    own_climate.wait()
    own_truth.wait()
    for s in range(2):
        if s == 1:
            other_truth.wait_recv()
        for lo, hi in spans:
            t = jnp.dot(pick[...], tbuf[s, :, lo:hi], preferred_element_type=F32)
            clim = jnp.dot(pick_c[...], cbuf[:, lo:hi], preferred_element_type=F32)
            actual[s, :, lo:hi] = t
            anomaly[s, :, lo:hi] = t - clim

    @pl.when(not_first)
    def _():
        edges[0].wait_recv()
        edges[2].wait_recv()

    @pl.when(not_last)
    def _():
        edges[1].wait_recv()
        edges[3].wait_recv()

    @pl.when(band == 0)
    def _():
        crs[:, 0] = jnp.zeros((2, 48, 384), BF16)

    @pl.when(band == bands - 1)
    def _():
        crs[:, 3] = jnp.zeros((2, 48, 384), BF16)

    swap.wait_recv()
    zmask = (lax.broadcasted_iota(jnp.int32, (8, 384), 0) // 2) % 2 == 0
    for s in range(2):
        planes = []
        for pair in range(4):
            both = crs[s, pair].astype(F32)
            planes += [both[0:24], both[24:48]]

        def put(at_row, value):
            high = value.astype(BF16)
            low = (value - high.astype(F32)).astype(BF16)
            rows = value.shape[0]
            fields[0, s, at_row : at_row + rows, :] = high
            fields[1, s, at_row : at_row + rows, :] = low

        for d in range(2):
            for xx in range(4):
                pieces = []
                for z in range(2):
                    total = None
                    for j in range(5):
                        c = 2 * z + xx // 2 + j
                        term = stencil[xx, z, c] * planes[c][8 * d : 8 * d + 8]
                        total = term if total is None else total + term
                    pieces.append(total)
                put(d * 64 + xx * 16, jnp.concatenate(pieces, axis=0))
        for pairx in range(2):
            pieces = []
            for xx in (2 * pairx, 2 * pairx + 1):
                total = None
                for c in range(8):
                    w0, w1 = stencil.get((xx, 0, c)), stencil.get((xx, 1, c))
                    if w0 is None and w1 is None:
                        continue
                    w = jnp.where(zmask, 0.0 if w0 is None else w0, 0.0 if w1 is None else w1)
                    term = w * planes[c][16:24]
                    total = term if total is None else total + term
                pieces.append(total)
            put(128 + 16 * pairx, jnp.concatenate(pieces, axis=0))

    going, staying = 1 - half, half
    even = lax.broadcasted_iota(jnp.int32, (8, 256), 0) % 4 < 2

    def coded(block):
        tiles = [block[:, 0:128], block[:, 128:256]]
        return encode(
            [t[r : r + 8] for r in (0, 16) for t in tiles],
            [t[r : r + 8] for r in (8, 24) for t in tiles],
            [t[32:40] for t in tiles],
        )

    def plain(words):
        sqs, ans, tails = decode(words, 4, 2)
        rows = [jnp.concatenate(g, axis=1) for g in (sqs[0:2], ans[0:2], sqs[2:4], ans[2:4], tails)]
        return jnp.concatenate(rows, axis=0)

    def hand_over(which, rows, ch):
        copies = {}
        for k in (1, 0, 2):
            xsend[k, which, ch] = coded(parts[(x + k + 1) % 4, rows, ch])
            copies[k] = send(
                xsend.at[k, which, ch],
                xrecv.at[k, which, ch],
                xssem.at[k, which, ch],
                xrsem.at[k, which, ch],
                across[k],
            )
        return copies

    def collect(which, rows, ch, copies):
        total = parts[x, rows, ch]
        for k in range(3):
            copies[k].wait_recv()
            total += plain(xrecv[k, which, ch])
        return total

    first, second = [], []
    for ch, (lo, hi) in enumerate(spans):
        width = hi - lo
        w = table[:, lo:hi]
        sq = an = None
        for s in range(2):
            fine = jnp.dot(fields[0, s], w, preferred_element_type=F32)
            fine += jnp.dot(fields[1, s], w, preferred_element_type=F32)
            error = fine - actual[s, :, lo:hi]
            true_anomaly = anomaly[s, :, lo:hi]
            e2 = error * error
            ab = (error + true_anomaly) * true_anomaly
            sq = e2 if sq is None else sq + e2
            an = ab if an is None else an + ab
        upper = lax.broadcasted_iota(jnp.int32, (8, width), 0) < 4
        for xx in range(4):
            tail = slice(128 + 8 * xx, 136 + 8 * xx)
            both = [t + pltpu.roll(t, 4, 0) for t in (sq[tail], an[tail])]
            mixed[ch, xx, :, 0:width] = jnp.where(upper, both[0], both[1])
            left, right = mixed[ch, xx, :, 0:256], mixed[ch, xx, :, 256:512]
            parts[xx, 0, ch, 32:40] = jnp.where(even, left, pltpu.roll(right, 2, 0))
            parts[xx, 1, ch, 32:40] = jnp.where(even, pltpu.roll(left, 6, 0), right)
            for z in range(2):
                r = 16 * xx + 8 * z
                for i, t in enumerate((sq, an)):
                    value = t[r : r + 8] + t[64 + r : 72 + r]
                    parts[xx, z, ch, 8 * i : 8 * i + 8] = value[:, 0:256]
                    parts[xx, z, ch, 16 + 8 * i : 24 + 8 * i, 0 : width - 256] = value[:, 256:width]
        first.append(hand_over(0, going, ch))

    zcopies = []
    for ch in range(CHUNKS):
        zsend[ch] = coded(collect(0, going, ch, first[ch]))
        if ch == 0:
            pl.when(half == 0)(lambda: pl.semaphore_wait(far_in, 1))
        zcopies.append(send(zsend.at[ch], zrecv.at[ch], zssem.at[ch], zrsem.at[ch], far))

    for ch in range(CHUNKS):
        second.append(hand_over(1, staying, ch))

    for ch in range(CHUNKS):
        zown[ch] = collect(1, staying, ch, second[ch])

    for ch, (start, _) in enumerate(spans):
        zcopies[ch].wait_recv()
        total = (zown[ch] + plain(zrecv[ch])) * (1.0 / 32.0)
        for side in range(2):
            lo = start + side * 256
            hi = min(lo + 256, WIDE)
            width = hi - lo
            for which in range(2):
                r = 16 * side + 8 * which
                out[which, 0:8, 0, lo:hi] = total[r : r + 8, 0:width]
                r = 32 + 4 * which + 2 * side
                out[which, 8:10, 0, lo:hi] = total[r : r + 2, 0:width]

    for copy in pending:
        copy.wait_send()

    @pl.when(not_last)
    def _():
        edges[0].wait_send()
        edges[2].wait_send()

    @pl.when(not_first)
    def _():
        edges[1].wait_send()
        edges[3].wait_send()


def shards(model, truth, climate, starts, lat_w, lon_first, lon_w):
    vmem = pl.BlockSpec(memory_space=pltpu.VMEM)
    hbm = pl.BlockSpec(memory_space=pl.ANY)
    maps = pl.pallas_call(
        kernel,
        out_shape=jax.ShapeDtypeStruct((2, 10, 1, WIDE), F32),
        in_specs=[hbm] * 7,
        out_specs=vmem,
        scratch_shapes=[
            pltpu.SMEM((16,), jnp.int32),
            pltpu.SMEM((4, 16), F32),
            pltpu.VMEM((WIDE,), jnp.int32),
            pltpu.VMEM((4, WIDE), BF16),
            pltpu.VMEM((20, 4, COARSE), BF16),
            pltpu.VMEM((2, 320, WIDE), BF16),
            pltpu.VMEM((160, WIDE), BF16),
            pltpu.VMEM((2, 4, 48, 384), BF16),
            pltpu.VMEM((2, 2, 160, 384), BF16),
            pltpu.VMEM((384, WIDE), BF16),
            pltpu.VMEM((160, 320), BF16),
            pltpu.VMEM((160, 160), BF16),
            pltpu.VMEM((2, 160, WIDE), F32),
            pltpu.VMEM((2, 160, WIDE), F32),
            pltpu.VMEM((CHUNKS, 4, 8, CHUNK), F32),
            pltpu.VMEM((4, 2, CHUNKS, 40, 256), F32),
            pltpu.VMEM((3, 2, CHUNKS, 48, 128), jnp.int32),
            pltpu.VMEM((3, 2, CHUNKS, 48, 128), jnp.int32),
            pltpu.VMEM((CHUNKS, 48, 128), jnp.int32),
            pltpu.VMEM((CHUNKS, 40, 256), F32),
            pltpu.VMEM((CHUNKS, 48, 128), jnp.int32),
            pltpu.SemaphoreType.DMA((7,)),
            pltpu.SemaphoreType.DMA((2,)),
            pltpu.SemaphoreType.DMA((5,)),
            pltpu.SemaphoreType.DMA((5,)),
            pltpu.SemaphoreType.DMA((3, 2, CHUNKS)),
            pltpu.SemaphoreType.DMA((3, 2, CHUNKS)),
            pltpu.SemaphoreType.DMA((CHUNKS,)),
            pltpu.SemaphoreType.DMA((CHUNKS,)),
            pltpu.SemaphoreType.REGULAR,
        ],
        compiler_params=pltpu.CompilerParams(
            collective_id=0, has_side_effects=True, vmem_limit_bytes=48 * 2**20
        ),
    )(
        *(
            pltpu.with_memory_space_constraint(operand, pltpu.HBM)
            for operand in (
                model.reshape(20, 4, COARSE),
                truth.reshape(320, WIDE),
                climate.reshape(160, WIDE),
                starts,
                lat_w.T,
                lon_first,
                lon_w,
            )
        )
    )
    return maps[0].reshape(2, 5, 1, WIDE), maps[1].reshape(2, 5, 1, WIDE)


def solution(mesh):
    in_specs = (
        P("date", None, None, "band", None),
        P("date", None, None, "band", None),
        P(None, None, "band", None),
        P("band"),
        P("band", None),
        P(),
        P(),
    )
    out_specs = (P(None, None, ("band", "date"), None), P(None, None, ("band", "date"), None))
    return jax.shard_map(shards, mesh=mesh, in_specs=in_specs, out_specs=out_specs, check_vma=False)
```

```python
import functools

import jax
import jax.numpy as jnp
from jax import lax
from jax.experimental import pallas as pl
from jax.experimental.pallas import tpu as pltpu
from jax.sharding import PartitionSpec as P

MESH = pl.DeviceIdType.MESH
F32 = jnp.float32
BF16 = jnp.bfloat16
WIDE = 1440
COARSE = 360
CHUNKS = 3
SPANS = ((0, 512, 256), (512, 1024, 256), (1024, 1440, 256))


def upper_rows():
    return lax.broadcasted_iota(jnp.int32, (8, 128), 0) < 4


def encode(sqs, ans, tails):
    upper = upper_rows()

    def scale(tiles, keep):
        most = functools.reduce(jnp.maximum, [jnp.abs(t) for t in tiles])
        more = functools.reduce(jnp.maximum, [jnp.abs(t) for t in tails])
        most = jnp.maximum(jnp.maximum(most, jnp.where(keep, more, 0.0)), 1e-25)
        most = jnp.max(most, axis=0, keepdims=True)
        return jnp.ceil(jnp.log(most) * (8.0 / 0.6931471805599453) + 0.01)

    e_sq, e_an = scale(sqs, upper), scale(ans, jnp.logical_not(upper))
    up_sq, up_an = (32767.0 * jnp.exp2(e * -0.125) for e in (e_sq, e_an))
    up_tail = jnp.where(upper, up_sq, up_an)
    words = []
    for tiles, up in ((sqs, up_sq), (ans, up_an), (tails, up_tail)):
        codes = [jnp.round(t * up).astype(jnp.int32) for t in tiles]
        if len(codes) % 2:
            odd = codes.pop()
            codes += [odd[0:4], odd[4:8]]
        for low, high in zip(codes[0::2], codes[1::2], strict=True):
            words.append((high << 16) | (low & 0xFFFF))
    words.append((e_sq.astype(jnp.int32) << 16) | (e_an.astype(jnp.int32) & 0xFFFF))
    return jnp.concatenate(words, axis=0)


def decode(words, n, n_tail):
    def both(t):
        return ((t << 16) >> 16).astype(F32), (t >> 16).astype(F32)

    last = words.shape[0] - 1
    e_an, e_sq = both(words[last : last + 1])
    down_sq, down_an = (jnp.exp2(e * 0.125) * (1.0 / 32767.0) for e in (e_sq, e_an))
    down_tail = jnp.where(upper_rows(), down_sq, down_an)
    values = []
    for i in range(n):
        down = down_sq if i < n // 2 else down_an
        values += [v * down for v in both(words[8 * i : 8 * i + 8])]
    tails = []
    for i in range(n, n + n_tail // 2):
        tails += [v * down_tail for v in both(words[8 * i : 8 * i + 8])]
    if n_tail % 2:
        tails.append(jnp.concatenate(both(words[last - 4 : last]), axis=0) * down_tail)
    return values[:n], values[n:], tails


def kernel(
    model, truth, climate, starts_in, lat_w_in, lon_first_in, lon_w_in,
    out,
    starts, lat_w, lon_first, lon_w, mbuf, tbuf, cbuf, crs, fields, table, pick, pick_c, actual, anomaly, mixed, parts, xsend, xrecv, zsend, zown, zrecv,
    lsem, tsem, csend, crecv, xssem, xrsem, zssem, zrsem, far_in,
):
    date = lax.axis_index("date")
    band = lax.axis_index("band")
    bands = 32
    half = date // 8
    x = (date // 2) % 4
    core = date % 2

    def at(h, xx, c):
        return h * 8 + xx * 2 + c

    sibling = (at(half, x, 1 - core), band)
    across = [(at(half, (x + k) % 4, core), band) for k in (1, 2, 3)]
    far = (at(1 - half, x, core), band)
    up, down = band + 1, band - 1
    near = [(date, up), (date, down), (at(half, x, 1 - core), up), (at(half, x, 1 - core), down)]
    not_last, not_first = band < bands - 1, band > 0
    barrier = pltpu.get_barrier_semaphore()

    def greet(partner):
        pl.semaphore_signal(barrier, inc=1, device_id=partner, device_id_type=MESH)

    pl.when(half == 0)(lambda: greet(far))
    pl.when(not_last)(lambda: [greet(near[0]), greet(near[2])] and None)
    pl.when(not_first)(lambda: [greet(near[1]), greet(near[3])] and None)
    for partner in [sibling] + across:
        greet(partner)

    own_model = pltpu.make_async_copy(model, mbuf, lsem.at[2])
    own_model.start()
    own_truth = pltpu.make_async_copy(truth, tbuf.at[0], lsem.at[0])
    own_truth.start()
    own_climate = pltpu.make_async_copy(climate, cbuf, lsem.at[1])
    own_climate.start()
    small = [
        pltpu.make_async_copy(source, target, lsem.at[3 + i])
        for i, (source, target) in enumerate(
            [(starts_in, starts), (lat_w_in, lat_w), (lon_first_in, lon_first), (lon_w_in, lon_w)]
        )
    ]
    for copy in small:
        copy.start()

    crs[0, 1:3] = jnp.zeros((2, 48, 384), BF16)
    own_model.wait()
    m = mbuf[...].astype(F32)
    for pair in range(2):
        rows = []
        for k in (2 * pair, 2 * pair + 1):
            plane = m[:, k, :]
            rows += [plane[0:8], plane[10:18]]
            a, b = plane[8:10], plane[18:20]
            rows += [a, a, b, b]
        crs[0, 1 + pair, :, 0:COARSE] = jnp.concatenate(rows, axis=0).astype(BF16)
    pl.semaphore_wait(
        barrier,
        4 + half + 2 * jnp.where(not_last, 1, 0) + 2 * jnp.where(not_first, 1, 0),
    )

    pending = []

    def make(src, dst, ssem, rsem, device):
        return pltpu.make_async_remote_copy(
            src_ref=src, dst_ref=dst, send_sem=ssem, recv_sem=rsem, device_id=device, device_id_type=MESH
        )

    def send(*what):
        copy = make(*what)
        copy.start()
        pending.append(copy)
        return copy

    edges = [
        make(crs.at[0, 2], crs.at[0, 0], csend.at[0], crecv.at[0], near[0]),
        make(crs.at[0, 1], crs.at[0, 3], csend.at[1], crecv.at[1], near[1]),
        make(crs.at[0, 2], crs.at[1, 0], csend.at[2], crecv.at[2], near[2]),
        make(crs.at[0, 1], crs.at[1, 3], csend.at[3], crecv.at[3], near[3]),
    ]

    @pl.when(not_last)
    def _():
        edges[0].start()
        edges[2].start()

    @pl.when(not_first)
    def _():
        edges[1].start()
        edges[3].start()

    swap = send(crs.at[0, pl.ds(1, 2)], crs.at[1, pl.ds(1, 2)], csend.at[4], crecv.at[4], sibling)

    @pl.when(half == 1)
    def _():
        pl.semaphore_signal(far_in, inc=1, device_id=far, device_id_type=MESH)

    other_truth = send(truth, tbuf.at[1], tsem.at[0], tsem.at[1], sibling)

    for copy in small:
        copy.wait()
    first_all = lon_first[...].reshape(1, WIDE)
    weights_all = lon_w[...].astype(F32)
    for start in range(0, WIDE, 512):
        width = min(512, WIDE - start)
        first = first_all[:, start : start + width]
        step = lax.broadcasted_iota(jnp.int32, (384, width), 0) - first
        step = jnp.where(step < 0, step + COARSE, step)
        block = jnp.zeros((384, width), F32)
        for k in range(4):
            block = jnp.where(step == k, weights_all[k : k + 1, start : start + width], block)
        row = lax.broadcasted_iota(jnp.int32, (384, width), 0)
        table[:, start : start + width] = jnp.where(row < COARSE, block, 0.0).astype(BF16)

    row = lax.broadcasted_iota(jnp.int32, (160, 1), 0)
    q = row - 128
    main = row < 128
    d_of = jnp.where(main, row // 64, (q % 8) // 4)
    x_of = jnp.where(main, (row % 64) // 16, q // 8)
    z_of = jnp.where(main, (row // 8) % 2, (q // 2) % 2)
    v_of = jnp.where(main, row % 8, 8 + q % 2)
    target = v_of * 16 + 8 * z_of + 2 * x_of + core
    column = lax.broadcasted_iota(jnp.int32, (160, 160), 1)
    pick_c[...] = (column == target).astype(F32).astype(BF16)
    column = lax.broadcasted_iota(jnp.int32, (160, 320), 1)
    pick[...] = (column == d_of * 160 + target).astype(F32).astype(BF16)
    for ch, (lo, hi, side) in enumerate(SPANS):
        if hi - lo < 2 * side:
            mixed[ch][:, :, side:] = jnp.zeros((4, 8, side), F32)
            parts[ch][:, :, 16:32] = jnp.zeros((4, 2, 16, side), F32)

    stencil = {}
    for xx in range(4):
        for z in range(2):
            r = 8 * z + 2 * xx + core
            base = 2 * z + xx // 2
            late = starts[r] - (4 * band + base - 2)
            w = [lat_w[k, r] for k in range(4)]
            five = [jnp.where(late == 0, w[0], 0.0)]
            five += [jnp.where(late == 0, w[j], w[j - 1]) for j in (1, 2, 3)]
            five += [jnp.where(late == 0, 0.0, w[3])]
            for j in range(5):
                stencil[xx, z, base + j] = five[j]

    spans = [(lo, min(lo + 512, WIDE)) for lo in range(0, WIDE, 512)]
    own_climate.wait()
    own_truth.wait()
    for s in range(2):
        if s == 1:
            other_truth.wait_recv()
        for lo, hi in spans:
            t = jnp.dot(pick[...], tbuf[s, :, lo:hi], preferred_element_type=F32)
            clim = jnp.dot(pick_c[...], cbuf[:, lo:hi], preferred_element_type=F32)
            actual[s, :, lo:hi] = t
            anomaly[s, :, lo:hi] = t - clim

    @pl.when(not_first)
    def _():
        edges[0].wait_recv()
        edges[2].wait_recv()

    @pl.when(not_last)
    def _():
        edges[1].wait_recv()
        edges[3].wait_recv()

    @pl.when(band == 0)
    def _():
        crs[:, 0] = jnp.zeros((2, 48, 384), BF16)

    @pl.when(band == bands - 1)
    def _():
        crs[:, 3] = jnp.zeros((2, 48, 384), BF16)

    swap.wait_recv()
    zmask = (lax.broadcasted_iota(jnp.int32, (8, 384), 0) // 2) % 2 == 0
    for s in range(2):
        planes = []
        for pair in range(4):
            both = crs[s, pair].astype(F32)
            planes += [both[0:24], both[24:48]]

        def put(at_row, value):
            high = value.astype(BF16)
            low = (value - high.astype(F32)).astype(BF16)
            rows = value.shape[0]
            fields[0, s, at_row : at_row + rows, :] = high
            fields[1, s, at_row : at_row + rows, :] = low

        for d in range(2):
            for xx in range(4):
                pieces = []
                for z in range(2):
                    total = None
                    for j in range(5):
                        c = 2 * z + xx // 2 + j
                        term = stencil[xx, z, c] * planes[c][8 * d : 8 * d + 8]
                        total = term if total is None else total + term
                    pieces.append(total)
                put(d * 64 + xx * 16, jnp.concatenate(pieces, axis=0))
        for pairx in range(2):
            pieces = []
            for xx in (2 * pairx, 2 * pairx + 1):
                total = None
                for c in range(8):
                    w0, w1 = stencil.get((xx, 0, c)), stencil.get((xx, 1, c))
                    if w0 is None and w1 is None:
                        continue
                    w = jnp.where(zmask, 0.0 if w0 is None else w0, 0.0 if w1 is None else w1)
                    term = w * planes[c][16:24]
                    total = term if total is None else total + term
                pieces.append(total)
            put(128 + 16 * pairx, jnp.concatenate(pieces, axis=0))

    going, staying = 1 - half, half

    def coded(block):
        tiles = [block[:, j : j + 128] for j in range(0, block.shape[1], 128)]
        return encode(
            [t[r : r + 8] for r in (0, 16) for t in tiles],
            [t[r : r + 8] for r in (8, 24) for t in tiles],
            [t[32:40] for t in tiles],
        )

    def plain(words):
        n = words.shape[0] // 20
        sqs, ans, tails = decode(words, 2 * n, n)
        rows = [jnp.concatenate(g, axis=1) for g in (sqs[:n], ans[:n], sqs[n:], ans[n:], tails)]
        return jnp.concatenate(rows, axis=0)

    def hand_over(which, rows, ch):
        copies = {}
        for k in (1, 0, 2):
            xsend[ch][k, which] = coded(parts[ch][(x + k + 1) % 4, rows])
            copies[k] = send(
                xsend[ch].at[k, which],
                xrecv[ch].at[k, which],
                xssem.at[k, which, ch],
                xrsem.at[k, which, ch],
                across[k],
            )
        return copies

    def collect(which, rows, ch, copies):
        total = parts[ch][x, rows]
        for k in range(3):
            copies[k].wait_recv()
            total += plain(xrecv[ch][k, which])
        return total

    first, second = [], []
    for ch, (lo, hi, side) in enumerate(SPANS):
        width = hi - lo
        even = lax.broadcasted_iota(jnp.int32, (8, side), 0) % 4 < 2
        w = table[:, lo:hi]
        sq = an = None
        for s in range(2):
            fine = jnp.dot(fields[0, s], w, preferred_element_type=F32)
            fine += jnp.dot(fields[1, s], w, preferred_element_type=F32)
            error = fine - actual[s, :, lo:hi]
            true_anomaly = anomaly[s, :, lo:hi]
            e2 = error * error
            ab = (error + true_anomaly) * true_anomaly
            sq = e2 if sq is None else sq + e2
            an = ab if an is None else an + ab
        upper = lax.broadcasted_iota(jnp.int32, (8, width), 0) < 4
        for xx in range(4):
            tail = slice(128 + 8 * xx, 136 + 8 * xx)
            both = [t + pltpu.roll(t, 4, 0) for t in (sq[tail], an[tail])]
            mixed[ch][xx, :, 0:width] = jnp.where(upper, both[0], both[1])
            left, right = mixed[ch][xx, :, 0:side], mixed[ch][xx, :, side:]
            parts[ch][xx, 0, 32:40] = jnp.where(even, left, pltpu.roll(right, 2, 0))
            parts[ch][xx, 1, 32:40] = jnp.where(even, pltpu.roll(left, 6, 0), right)
            for z in range(2):
                r = 16 * xx + 8 * z
                for i, t in enumerate((sq, an)):
                    value = t[r : r + 8] + t[64 + r : 72 + r]
                    parts[ch][xx, z, 8 * i : 8 * i + 8] = value[:, 0:side]
                    parts[ch][xx, z, 16 + 8 * i : 24 + 8 * i, 0 : width - side] = value[:, side:width]
        first.append(hand_over(0, going, ch))

    zcopies = []
    for ch in range(CHUNKS):
        zsend[ch][...] = coded(collect(0, going, ch, first[ch]))
        if ch == 0:
            pl.when(half == 0)(lambda: pl.semaphore_wait(far_in, 1))
        zcopies.append(send(zsend[ch], zrecv[ch], zssem.at[ch], zrsem.at[ch], far))

    for ch in range(CHUNKS):
        second.append(hand_over(1, staying, ch))

    for ch in range(CHUNKS):
        zown[ch][...] = collect(1, staying, ch, second[ch])

    for ch, (start, stop, half_width) in enumerate(SPANS):
        zcopies[ch].wait_recv()
        total = (zown[ch][...] + plain(zrecv[ch][...])) * (1.0 / 32.0)
        for side in range(2):
            lo = start + side * half_width
            hi = min(lo + half_width, stop)
            width = hi - lo
            for which in range(2):
                r = 16 * side + 8 * which
                out[which, 0:8, 0, lo:hi] = total[r : r + 8, 0:width]
                r = 32 + 4 * which + 2 * side
                out[which, 8:10, 0, lo:hi] = total[r : r + 2, 0:width]

    for copy in pending:
        copy.wait_send()

    @pl.when(not_last)
    def _():
        edges[0].wait_send()
        edges[2].wait_send()

    @pl.when(not_first)
    def _():
        edges[1].wait_send()
        edges[3].wait_send()


def per_chunk(buffer):
    return [buffer(side, 20 * (side // 128) + 1) for _, _, side in SPANS]


def shards(model, truth, climate, starts, lat_w, lon_first, lon_w):
    vmem = pl.BlockSpec(memory_space=pltpu.VMEM)
    hbm = pl.BlockSpec(memory_space=pl.ANY)
    maps = pl.pallas_call(
        kernel,
        out_shape=jax.ShapeDtypeStruct((2, 10, 1, WIDE), F32),
        in_specs=[hbm] * 7,
        out_specs=vmem,
        scratch_shapes=[
            pltpu.SMEM((16,), jnp.int32),
            pltpu.SMEM((4, 16), F32),
            pltpu.VMEM((WIDE,), jnp.int32),
            pltpu.VMEM((4, WIDE), BF16),
            pltpu.VMEM((20, 4, COARSE), BF16),
            pltpu.VMEM((2, 320, WIDE), BF16),
            pltpu.VMEM((160, WIDE), BF16),
            pltpu.VMEM((2, 4, 48, 384), BF16),
            pltpu.VMEM((2, 2, 160, 384), BF16),
            pltpu.VMEM((384, WIDE), BF16),
            pltpu.VMEM((160, 320), BF16),
            pltpu.VMEM((160, 160), BF16),
            pltpu.VMEM((2, 160, WIDE), F32),
            pltpu.VMEM((2, 160, WIDE), F32),
            per_chunk(lambda side, rows: pltpu.VMEM((4, 8, 2 * side), F32)),
            per_chunk(lambda side, rows: pltpu.VMEM((4, 2, 40, side), F32)),
            per_chunk(lambda side, rows: pltpu.VMEM((3, 2, rows, 128), jnp.int32)),
            per_chunk(lambda side, rows: pltpu.VMEM((3, 2, rows, 128), jnp.int32)),
            per_chunk(lambda side, rows: pltpu.VMEM((rows, 128), jnp.int32)),
            per_chunk(lambda side, rows: pltpu.VMEM((40, side), F32)),
            per_chunk(lambda side, rows: pltpu.VMEM((rows, 128), jnp.int32)),
            pltpu.SemaphoreType.DMA((7,)),
            pltpu.SemaphoreType.DMA((2,)),
            pltpu.SemaphoreType.DMA((5,)),
            pltpu.SemaphoreType.DMA((5,)),
            pltpu.SemaphoreType.DMA((3, 2, CHUNKS)),
            pltpu.SemaphoreType.DMA((3, 2, CHUNKS)),
            pltpu.SemaphoreType.DMA((CHUNKS,)),
            pltpu.SemaphoreType.DMA((CHUNKS,)),
            pltpu.SemaphoreType.REGULAR,
        ],
        compiler_params=pltpu.CompilerParams(
            collective_id=0, has_side_effects=True, vmem_limit_bytes=48 * 2**20
        ),
    )(
        *(
            pltpu.with_memory_space_constraint(operand, pltpu.HBM)
            for operand in (
                model.reshape(20, 4, COARSE),
                truth.reshape(320, WIDE),
                climate.reshape(160, WIDE),
                starts,
                lat_w.T,
                lon_first,
                lon_w,
            )
        )
    )
    return maps[0].reshape(2, 5, 1, WIDE), maps[1].reshape(2, 5, 1, WIDE)


def solution(mesh):
    in_specs = (
        P("date", None, None, "band", None),
        P("date", None, None, "band", None),
        P(None, None, "band", None),
        P("band"),
        P("band", None),
        P(),
        P(),
    )
    out_specs = (P(None, None, ("band", "date"), None), P(None, None, ("band", "date"), None))
    return jax.shard_map(shards, mesh=mesh, in_specs=in_specs, out_specs=out_specs, check_vma=False)
```

```python
import functools

import jax
import jax.numpy as jnp
from jax import lax
from jax.experimental import pallas as pl
from jax.experimental.pallas import tpu as pltpu
from jax.sharding import PartitionSpec as P

MESH = pl.DeviceIdType.MESH
F32 = jnp.float32
BF16 = jnp.bfloat16
WIDE = 1440
COARSE = 360
CHUNKS = 3
SPANS = ((0, 512, 256), (512, 1024, 256), (1024, 1440, 256))


def upper_rows():
    return lax.broadcasted_iota(jnp.int32, (8, 128), 0) < 4


def encode(sqs, ans, tails):
    upper = upper_rows()

    def scale(tiles, keep):
        most = functools.reduce(jnp.maximum, [jnp.abs(t) for t in tiles])
        more = functools.reduce(jnp.maximum, [jnp.abs(t) for t in tails])
        most = jnp.maximum(jnp.maximum(most, jnp.where(keep, more, 0.0)), 1e-25)
        most = jnp.max(most, axis=0, keepdims=True)
        return jnp.ceil(jnp.log(most) * (8.0 / 0.6931471805599453) + 0.01)

    e_sq, e_an = scale(sqs, upper), scale(ans, jnp.logical_not(upper))
    up_sq, up_an = (32767.0 * jnp.exp2(e * -0.125) for e in (e_sq, e_an))
    up_tail = jnp.where(upper, up_sq, up_an)
    words = []
    for tiles, up in ((sqs, up_sq), (ans, up_an), (tails, up_tail)):
        codes = [jnp.round(t * up).astype(jnp.int32) for t in tiles]
        if len(codes) % 2:
            odd = codes.pop()
            codes += [odd[0:4], odd[4:8]]
        for low, high in zip(codes[0::2], codes[1::2], strict=True):
            words.append((high << 16) | (low & 0xFFFF))
    words.append((e_sq.astype(jnp.int32) << 16) | (e_an.astype(jnp.int32) & 0xFFFF))
    return jnp.concatenate(words, axis=0)


def decode(words, n, n_tail):
    def both(t):
        return ((t << 16) >> 16).astype(F32), (t >> 16).astype(F32)

    last = words.shape[0] - 1
    e_an, e_sq = both(words[last : last + 1])
    down_sq, down_an = (jnp.exp2(e * 0.125) * (1.0 / 32767.0) for e in (e_sq, e_an))
    down_tail = jnp.where(upper_rows(), down_sq, down_an)
    values = []
    for i in range(n):
        down = down_sq if i < n // 2 else down_an
        values += [v * down for v in both(words[8 * i : 8 * i + 8])]
    tails = []
    for i in range(n, n + n_tail // 2):
        tails += [v * down_tail for v in both(words[8 * i : 8 * i + 8])]
    if n_tail % 2:
        tails.append(jnp.concatenate(both(words[last - 4 : last]), axis=0) * down_tail)
    return values[:n], values[n:], tails


def kernel(
    model, truth, climate, starts_in, lat_w_in, lon_first_in, lon_w_in,
    out,
    starts, lat_w, lon_first, lon_w, mbuf, tbuf, cbuf, crs, fields, table, pick, pick_c, inner, actual, anomaly, mixed, parts, xsend, xrecv, zsend, zown, zrecv,
    lsem, tsem, csend, crecv, xssem, xrsem, zssem, zrsem, far_in,
):
    date = lax.axis_index("date")
    band = lax.axis_index("band")
    bands = 32
    half = date // 8
    x = (date // 2) % 4
    core = date % 2

    def at(h, xx, c):
        return h * 8 + xx * 2 + c

    sibling = (at(half, x, 1 - core), band)
    across = [(at(half, (x + k) % 4, core), band) for k in (1, 2, 3)]
    far = (at(1 - half, x, core), band)
    up, down = band + 1, band - 1
    near = [(date, up), (date, down), (at(half, x, 1 - core), up), (at(half, x, 1 - core), down)]
    not_last, not_first = band < bands - 1, band > 0
    barrier = pltpu.get_barrier_semaphore()

    def greet(partner):
        pl.semaphore_signal(barrier, inc=1, device_id=partner, device_id_type=MESH)

    pl.when(half == 0)(lambda: greet(far))
    pl.when(not_last)(lambda: [greet(near[0]), greet(near[2])] and None)
    pl.when(not_first)(lambda: [greet(near[1]), greet(near[3])] and None)
    for partner in [sibling] + across:
        greet(partner)

    own_model = pltpu.make_async_copy(model, mbuf, lsem.at[2])
    own_model.start()
    own_truth = pltpu.make_async_copy(truth, tbuf.at[0], lsem.at[0])
    own_truth.start()
    own_climate = pltpu.make_async_copy(climate, cbuf, lsem.at[1])
    own_climate.start()
    small = [
        pltpu.make_async_copy(source, target, lsem.at[3 + i])
        for i, (source, target) in enumerate(
            [(starts_in, starts), (lat_w_in, lat_w), (lon_first_in, lon_first), (lon_w_in, lon_w)]
        )
    ]
    for copy in small:
        copy.start()

    crs[0, 1:3] = jnp.zeros((2, 48, 384), BF16)
    own_model.wait()
    m = mbuf[...].astype(F32)
    for pair in range(2):
        rows = []
        for k in (2 * pair, 2 * pair + 1):
            plane = m[:, k, :]
            rows += [plane[0:8], plane[10:18]]
            a, b = plane[8:10], plane[18:20]
            rows += [a, a, b, b]
        crs[0, 1 + pair, :, 0:COARSE] = jnp.concatenate(rows, axis=0).astype(BF16)
    pl.semaphore_wait(
        barrier,
        4 + half + 2 * jnp.where(not_last, 1, 0) + 2 * jnp.where(not_first, 1, 0),
    )

    pending = []

    def make(src, dst, ssem, rsem, device):
        return pltpu.make_async_remote_copy(
            src_ref=src, dst_ref=dst, send_sem=ssem, recv_sem=rsem, device_id=device, device_id_type=MESH
        )

    def send(*what):
        copy = make(*what)
        copy.start()
        pending.append(copy)
        return copy

    edges = [
        make(crs.at[0, 2], crs.at[0, 0], csend.at[0], crecv.at[0], near[0]),
        make(crs.at[0, 1], crs.at[0, 3], csend.at[1], crecv.at[1], near[1]),
        make(crs.at[0, 2], crs.at[1, 0], csend.at[2], crecv.at[2], near[2]),
        make(crs.at[0, 1], crs.at[1, 3], csend.at[3], crecv.at[3], near[3]),
    ]

    @pl.when(not_last)
    def _():
        edges[0].start()
        edges[2].start()

    @pl.when(not_first)
    def _():
        edges[1].start()
        edges[3].start()

    swap = send(crs.at[0, pl.ds(1, 2)], crs.at[1, pl.ds(1, 2)], csend.at[4], crecv.at[4], sibling)

    @pl.when(half == 1)
    def _():
        pl.semaphore_signal(far_in, inc=1, device_id=far, device_id_type=MESH)

    other_truth = send(truth, tbuf.at[1], tsem.at[0], tsem.at[1], sibling)

    for copy in small:
        copy.wait()
    first_all = lon_first[...].reshape(1, WIDE)
    weights_all = lon_w[...].astype(F32)
    for start in range(0, WIDE, 512):
        width = min(512, WIDE - start)
        first = first_all[:, start : start + width]
        step = lax.broadcasted_iota(jnp.int32, (384, width), 0) - first
        step = jnp.where(step < 0, step + COARSE, step)
        block = jnp.zeros((384, width), F32)
        for k in range(4):
            block = jnp.where(step == k, weights_all[k : k + 1, start : start + width], block)
        row = lax.broadcasted_iota(jnp.int32, (384, width), 0)
        table[:, start : start + width] = jnp.where(row < COARSE, block, 0.0).astype(BF16)

    row = lax.broadcasted_iota(jnp.int32, (160, 1), 0)
    q = row - 128
    main = row < 128
    d_of = jnp.where(main, row // 64, (q % 8) // 4)
    x_of = jnp.where(main, (row % 64) // 16, q // 8)
    z_of = jnp.where(main, (row // 8) % 2, (q // 2) % 2)
    v_of = jnp.where(main, row % 8, 8 + q % 2)
    target = v_of * 16 + 8 * z_of + 2 * x_of + core
    column = lax.broadcasted_iota(jnp.int32, (160, 160), 1)
    pick_c[...] = (column == target).astype(F32).astype(BF16)
    column = lax.broadcasted_iota(jnp.int32, (160, 320), 1)
    pick[...] = (column == d_of * 160 + target).astype(F32).astype(BF16)
    for ch, (lo, hi, side) in enumerate(SPANS):
        if hi - lo < 2 * side:
            mixed[ch][:, :, side:] = jnp.zeros((4, 8, side), F32)
            parts[ch][:, :, 16:32] = jnp.zeros((4, 2, 16, side), F32)

    stencil = {}
    for xx in range(4):
        for z in range(2):
            r = 8 * z + 2 * xx + core
            base = 2 * z + xx // 2
            late = starts[r] - (4 * band + base - 2)
            w = [lat_w[k, r] for k in range(4)]
            five = [jnp.where(late == 0, w[0], 0.0)]
            five += [jnp.where(late == 0, w[j], w[j - 1]) for j in (1, 2, 3)]
            five += [jnp.where(late == 0, 0.0, w[3])]
            for j in range(5):
                stencil[xx, z, base + j] = five[j]

    spans = [(lo, min(lo + 512, WIDE)) for lo in range(0, WIDE, 512)]
    own_climate.wait()
    own_truth.wait()
    for s in range(2):
        if s == 1:
            other_truth.wait_recv()
        for lo, hi in spans:
            t = jnp.dot(pick[...], tbuf[s, :, lo:hi], preferred_element_type=F32)
            clim = jnp.dot(pick_c[...], cbuf[:, lo:hi], preferred_element_type=F32)
            actual[s, :, lo:hi] = t
            anomaly[s, :, lo:hi] = t - clim

    zmask = (lax.broadcasted_iota(jnp.int32, (8, 384), 0) // 2) % 2 == 0

    def stencil_sum(s, pairs):
        planes = {}
        for pair in pairs:
            both = crs[s, pair].astype(F32)
            planes[2 * pair], planes[2 * pair + 1] = both[0:24], both[24:48]

        def weigh(terms):
            terms = [w * v for w, v in terms]
            return functools.reduce(jnp.add, terms) if terms else None

        result = {}
        for xx in range(4):
            for d in range(2):
                for z in range(2):
                    reach = range(2 * z + xx // 2, 2 * z + xx // 2 + 5)
                    result[d * 64 + xx * 16 + z * 8] = weigh(
                        [(stencil[xx, z, c], planes[c][8 * d : 8 * d + 8]) for c in reach if c in planes]
                    )
            terms = []
            for c in planes:
                w0, w1 = stencil.get((xx, 0, c)), stencil.get((xx, 1, c))
                if w0 is not None or w1 is not None:
                    w = jnp.where(zmask, 0.0 if w0 is None else w0, 0.0 if w1 is None else w1)
                    terms.append((w, planes[c][16:24]))
            result[128 + 8 * xx] = weigh(terms)
        return result

    swap.wait_recv()
    for s in range(2):
        for r, value in stencil_sum(s, (1, 2)).items():
            inner[s, r : r + 8] = value

    @pl.when(not_first)
    def _():
        edges[0].wait_recv()
        edges[2].wait_recv()

    @pl.when(not_last)
    def _():
        edges[1].wait_recv()
        edges[3].wait_recv()

    @pl.when(band == 0)
    def _():
        crs[:, 0] = jnp.zeros((2, 48, 384), BF16)

    @pl.when(band == bands - 1)
    def _():
        crs[:, 3] = jnp.zeros((2, 48, 384), BF16)

    for s in range(2):
        edge = stencil_sum(s, (0, 3))
        for r in range(0, 160, 16):
            rows = []
            for q in (r, r + 8):
                rows.append(inner[s, q : q + 8] if edge[q] is None else inner[s, q : q + 8] + edge[q])
            value = jnp.concatenate(rows, axis=0)
            high = value.astype(BF16)
            fields[0, s, r : r + 16] = high
            fields[1, s, r : r + 16] = (value - high.astype(F32)).astype(BF16)

    going, staying = 1 - half, half

    def coded(block):
        tiles = [block[:, j : j + 128] for j in range(0, block.shape[1], 128)]
        return encode(
            [t[r : r + 8] for r in (0, 16) for t in tiles],
            [t[r : r + 8] for r in (8, 24) for t in tiles],
            [t[32:40] for t in tiles],
        )

    def plain(words):
        n = words.shape[0] // 20
        sqs, ans, tails = decode(words, 2 * n, n)
        rows = [jnp.concatenate(g, axis=1) for g in (sqs[:n], ans[:n], sqs[n:], ans[n:], tails)]
        return jnp.concatenate(rows, axis=0)

    def hand_over(which, rows, ch):
        copies = {}
        messages = [coded(parts[ch][(x + k + 1) % 4, rows]) for k in range(3)]
        for k in range(3):
            xsend[ch][k, which] = messages[k]
        for k in (1, 0, 2):
            copies[k] = send(
                xsend[ch].at[k, which],
                xrecv[ch].at[k, which],
                xssem.at[k, which, ch],
                xrsem.at[k, which, ch],
                across[k],
            )
        return copies

    def collect(which, rows, ch, copies):
        total = parts[ch][x, rows]
        for k in range(3):
            copies[k].wait_recv()
            total += plain(xrecv[ch][k, which])
        return total

    first, second = [], []
    for ch, (lo, hi, side) in enumerate(SPANS):
        width = hi - lo
        even = lax.broadcasted_iota(jnp.int32, (8, side), 0) % 4 < 2
        w = table[:, lo:hi]
        sq = an = None
        for s in range(2):
            fine = jnp.dot(fields[0, s], w, preferred_element_type=F32)
            fine += jnp.dot(fields[1, s], w, preferred_element_type=F32)
            error = fine - actual[s, :, lo:hi]
            true_anomaly = anomaly[s, :, lo:hi]
            e2 = error * error
            ab = (error + true_anomaly) * true_anomaly
            sq = e2 if sq is None else sq + e2
            an = ab if an is None else an + ab
        upper = lax.broadcasted_iota(jnp.int32, (8, width), 0) < 4
        for xx in range(4):
            tail = slice(128 + 8 * xx, 136 + 8 * xx)
            both = [t + pltpu.roll(t, 4, 0) for t in (sq[tail], an[tail])]
            mixed[ch][xx, :, 0:width] = jnp.where(upper, both[0], both[1])
            left, right = mixed[ch][xx, :, 0:side], mixed[ch][xx, :, side:]
            parts[ch][xx, 0, 32:40] = jnp.where(even, left, pltpu.roll(right, 2, 0))
            parts[ch][xx, 1, 32:40] = jnp.where(even, pltpu.roll(left, 6, 0), right)
            for z in range(2):
                r = 16 * xx + 8 * z
                for i, t in enumerate((sq, an)):
                    value = t[r : r + 8] + t[64 + r : 72 + r]
                    parts[ch][xx, z, 8 * i : 8 * i + 8] = value[:, 0:side]
                    parts[ch][xx, z, 16 + 8 * i : 24 + 8 * i, 0 : width - side] = value[:, side:width]
        first.append(hand_over(0, going, ch))

    zcopies = []
    for ch in range(CHUNKS):
        zsend[ch][...] = coded(collect(0, going, ch, first[ch]))
        if ch == 0:
            pl.when(half == 0)(lambda: pl.semaphore_wait(far_in, 1))
        zcopies.append(send(zsend[ch], zrecv[ch], zssem.at[ch], zrsem.at[ch], far))

    for ch in range(CHUNKS):
        second.append(hand_over(1, staying, ch))

    for ch in range(CHUNKS):
        zown[ch][...] = collect(1, staying, ch, second[ch])

    for ch, (start, stop, half_width) in enumerate(SPANS):
        zcopies[ch].wait_recv()
        total = (zown[ch][...] + plain(zrecv[ch][...])) * (1.0 / 32.0)
        for side in range(2):
            lo = start + side * half_width
            hi = min(lo + half_width, stop)
            width = hi - lo
            for which in range(2):
                r = 16 * side + 8 * which
                out[which, 0:8, 0, lo:hi] = total[r : r + 8, 0:width]
                r = 32 + 4 * which + 2 * side
                out[which, 8:10, 0, lo:hi] = total[r : r + 2, 0:width]

    for copy in pending:
        copy.wait_send()

    @pl.when(not_last)
    def _():
        edges[0].wait_send()
        edges[2].wait_send()

    @pl.when(not_first)
    def _():
        edges[1].wait_send()
        edges[3].wait_send()


def per_chunk(buffer):
    return [buffer(side, 20 * (side // 128) + 1) for _, _, side in SPANS]


def shards(model, truth, climate, starts, lat_w, lon_first, lon_w):
    vmem = pl.BlockSpec(memory_space=pltpu.VMEM)
    hbm = pl.BlockSpec(memory_space=pl.ANY)
    maps = pl.pallas_call(
        kernel,
        out_shape=jax.ShapeDtypeStruct((2, 10, 1, WIDE), F32),
        in_specs=[hbm] * 7,
        out_specs=vmem,
        scratch_shapes=[
            pltpu.SMEM((16,), jnp.int32),
            pltpu.SMEM((4, 16), F32),
            pltpu.VMEM((WIDE,), jnp.int32),
            pltpu.VMEM((4, WIDE), BF16),
            pltpu.VMEM((20, 4, COARSE), BF16),
            pltpu.VMEM((2, 320, WIDE), BF16),
            pltpu.VMEM((160, WIDE), BF16),
            pltpu.VMEM((2, 4, 48, 384), BF16),
            pltpu.VMEM((2, 2, 160, 384), BF16),
            pltpu.VMEM((384, WIDE), BF16),
            pltpu.VMEM((160, 320), BF16),
            pltpu.VMEM((160, 160), BF16),
            pltpu.VMEM((2, 160, 384), F32),
            pltpu.VMEM((2, 160, WIDE), F32),
            pltpu.VMEM((2, 160, WIDE), F32),
            per_chunk(lambda side, rows: pltpu.VMEM((4, 8, 2 * side), F32)),
            per_chunk(lambda side, rows: pltpu.VMEM((4, 2, 40, side), F32)),
            per_chunk(lambda side, rows: pltpu.VMEM((3, 2, rows, 128), jnp.int32)),
            per_chunk(lambda side, rows: pltpu.VMEM((3, 2, rows, 128), jnp.int32)),
            per_chunk(lambda side, rows: pltpu.VMEM((rows, 128), jnp.int32)),
            per_chunk(lambda side, rows: pltpu.VMEM((40, side), F32)),
            per_chunk(lambda side, rows: pltpu.VMEM((rows, 128), jnp.int32)),
            pltpu.SemaphoreType.DMA((7,)),
            pltpu.SemaphoreType.DMA((2,)),
            pltpu.SemaphoreType.DMA((5,)),
            pltpu.SemaphoreType.DMA((5,)),
            pltpu.SemaphoreType.DMA((3, 2, CHUNKS)),
            pltpu.SemaphoreType.DMA((3, 2, CHUNKS)),
            pltpu.SemaphoreType.DMA((CHUNKS,)),
            pltpu.SemaphoreType.DMA((CHUNKS,)),
            pltpu.SemaphoreType.REGULAR,
        ],
        compiler_params=pltpu.CompilerParams(
            collective_id=0, has_side_effects=True, vmem_limit_bytes=48 * 2**20
        ),
    )(
        *(
            pltpu.with_memory_space_constraint(operand, pltpu.HBM)
            for operand in (
                model.reshape(20, 4, COARSE),
                truth.reshape(320, WIDE),
                climate.reshape(160, WIDE),
                starts,
                lat_w.T,
                lon_first,
                lon_w,
            )
        )
    )
    return maps[0].reshape(2, 5, 1, WIDE), maps[1].reshape(2, 5, 1, WIDE)


def solution(mesh):
    in_specs = (
        P("date", None, None, "band", None),
        P("date", None, None, "band", None),
        P(None, None, "band", None),
        P("band"),
        P("band", None),
        P(),
        P(),
    )
    out_specs = (P(None, None, ("band", "date"), None), P(None, None, ("band", "date"), None))
    return jax.shard_map(shards, mesh=mesh, in_specs=in_specs, out_specs=out_specs, check_vma=False)
```

```python
import functools

import jax
import jax.numpy as jnp
from jax import lax
from jax.experimental import pallas as pl
from jax.experimental.pallas import tpu as pltpu
from jax.sharding import PartitionSpec as P

MESH = pl.DeviceIdType.MESH
F32 = jnp.float32
BF16 = jnp.bfloat16
WIDE = 1440
COARSE = 360
CHUNKS = 3
SPANS = ((1024, 1440, 256), (0, 512, 256), (512, 1024, 256))


def upper_rows():
    return lax.broadcasted_iota(jnp.int32, (8, 128), 0) < 4


def encode(sqs, ans, tails):
    upper = upper_rows()

    def scale(tiles, keep):
        most = functools.reduce(jnp.maximum, [jnp.abs(t) for t in tiles])
        more = functools.reduce(jnp.maximum, [jnp.abs(t) for t in tails])
        most = jnp.maximum(jnp.maximum(most, jnp.where(keep, more, 0.0)), 1e-25)
        most = jnp.max(most, axis=0, keepdims=True)
        return jnp.ceil(jnp.log(most) * (8.0 / 0.6931471805599453) + 0.01)

    e_sq, e_an = scale(sqs, upper), scale(ans, jnp.logical_not(upper))
    up_sq, up_an = (32767.0 * jnp.exp2(e * -0.125) for e in (e_sq, e_an))
    up_tail = jnp.where(upper, up_sq, up_an)
    words = []
    for tiles, up in ((sqs, up_sq), (ans, up_an), (tails, up_tail)):
        codes = [jnp.round(t * up).astype(jnp.int32) for t in tiles]
        if len(codes) % 2:
            odd = codes.pop()
            codes += [odd[0:4], odd[4:8]]
        for low, high in zip(codes[0::2], codes[1::2], strict=True):
            words.append((high << 16) | (low & 0xFFFF))
    words.append((e_sq.astype(jnp.int32) << 16) | (e_an.astype(jnp.int32) & 0xFFFF))
    return jnp.concatenate(words, axis=0)


def decode(words, n, n_tail):
    def both(t):
        return ((t << 16) >> 16).astype(F32), (t >> 16).astype(F32)

    last = words.shape[0] - 1
    e_an, e_sq = both(words[last : last + 1])
    down_sq, down_an = (jnp.exp2(e * 0.125) * (1.0 / 32767.0) for e in (e_sq, e_an))
    down_tail = jnp.where(upper_rows(), down_sq, down_an)
    values = []
    for i in range(n):
        down = down_sq if i < n // 2 else down_an
        values += [v * down for v in both(words[8 * i : 8 * i + 8])]
    tails = []
    for i in range(n, n + n_tail // 2):
        tails += [v * down_tail for v in both(words[8 * i : 8 * i + 8])]
    if n_tail % 2:
        tails.append(jnp.concatenate(both(words[last - 4 : last]), axis=0) * down_tail)
    return values[:n], values[n:], tails


def kernel(
    model, truth, climate, starts_in, lat_w_in, lon_first_in, lon_w_in,
    out,
    starts, lat_w, lon_first, lon_w, mbuf, tbuf, cbuf, crs, fields, table, pick, pick_c, inner, actual, anomaly, mixed, parts, xsend, xrecv, zsend, zown, zrecv,
    lsem, tsem, csend, crecv, xssem, xrsem, zssem, zrsem, far_in,
):
    date = lax.axis_index("date")
    band = lax.axis_index("band")
    bands = 32
    half = date // 8
    x = (date // 2) % 4
    core = date % 2

    def at(h, xx, c):
        return h * 8 + xx * 2 + c

    sibling = (at(half, x, 1 - core), band)
    across = [(at(half, (x + k) % 4, core), band) for k in (1, 2, 3)]
    far = (at(1 - half, x, core), band)
    up, down = band + 1, band - 1
    near = [(date, up), (date, down), (at(half, x, 1 - core), up), (at(half, x, 1 - core), down)]
    not_last, not_first = band < bands - 1, band > 0
    barrier = pltpu.get_barrier_semaphore()

    def greet(partner):
        pl.semaphore_signal(barrier, inc=1, device_id=partner, device_id_type=MESH)

    pl.when(half == 0)(lambda: greet(far))
    pl.when(not_last)(lambda: [greet(near[0]), greet(near[2])] and None)
    pl.when(not_first)(lambda: [greet(near[1]), greet(near[3])] and None)
    for partner in [sibling] + across:
        greet(partner)

    own_model = pltpu.make_async_copy(model, mbuf, lsem.at[2])
    own_model.start()
    own_truth = pltpu.make_async_copy(truth, tbuf.at[0], lsem.at[0])
    own_truth.start()
    own_climate = pltpu.make_async_copy(climate, cbuf, lsem.at[1])
    own_climate.start()
    small = [
        pltpu.make_async_copy(source, target, lsem.at[3 + i])
        for i, (source, target) in enumerate(
            [(starts_in, starts), (lat_w_in, lat_w), (lon_first_in, lon_first), (lon_w_in, lon_w)]
        )
    ]
    for copy in small:
        copy.start()

    crs[0, 1:3] = jnp.zeros((2, 48, 384), BF16)
    own_model.wait()
    m = mbuf[...].astype(F32)
    for pair in range(2):
        rows = []
        for k in (2 * pair, 2 * pair + 1):
            plane = m[:, k, :]
            rows += [plane[0:8], plane[10:18]]
            a, b = plane[8:10], plane[18:20]
            rows += [a, a, b, b]
        crs[0, 1 + pair, :, 0:COARSE] = jnp.concatenate(rows, axis=0).astype(BF16)
    pl.semaphore_wait(
        barrier,
        4 + half + 2 * jnp.where(not_last, 1, 0) + 2 * jnp.where(not_first, 1, 0),
    )

    pending = []

    def make(src, dst, ssem, rsem, device):
        return pltpu.make_async_remote_copy(
            src_ref=src, dst_ref=dst, send_sem=ssem, recv_sem=rsem, device_id=device, device_id_type=MESH
        )

    def send(*what):
        copy = make(*what)
        copy.start()
        pending.append(copy)
        return copy

    edges = [
        make(crs.at[0, 2], crs.at[0, 0], csend.at[0], crecv.at[0], near[0]),
        make(crs.at[0, 1], crs.at[0, 3], csend.at[1], crecv.at[1], near[1]),
        make(crs.at[0, 2], crs.at[1, 0], csend.at[2], crecv.at[2], near[2]),
        make(crs.at[0, 1], crs.at[1, 3], csend.at[3], crecv.at[3], near[3]),
    ]

    @pl.when(not_last)
    def _():
        edges[0].start()
        edges[2].start()

    @pl.when(not_first)
    def _():
        edges[1].start()
        edges[3].start()

    swap = send(crs.at[0, pl.ds(1, 2)], crs.at[1, pl.ds(1, 2)], csend.at[4], crecv.at[4], sibling)

    @pl.when(half == 1)
    def _():
        pl.semaphore_signal(far_in, inc=1, device_id=far, device_id_type=MESH)

    other_truth = send(truth, tbuf.at[1], tsem.at[0], tsem.at[1], sibling)

    for copy in small:
        copy.wait()
    first_all = lon_first[...].reshape(1, WIDE)
    weights_all = lon_w[...].astype(F32)
    for start in range(0, WIDE, 512):
        width = min(512, WIDE - start)
        first = first_all[:, start : start + width]
        step = lax.broadcasted_iota(jnp.int32, (384, width), 0) - first
        step = jnp.where(step < 0, step + COARSE, step)
        block = jnp.zeros((384, width), F32)
        for k in range(4):
            block = jnp.where(step == k, weights_all[k : k + 1, start : start + width], block)
        row = lax.broadcasted_iota(jnp.int32, (384, width), 0)
        table[:, start : start + width] = jnp.where(row < COARSE, block, 0.0).astype(BF16)

    row = lax.broadcasted_iota(jnp.int32, (160, 1), 0)
    q = row - 128
    main = row < 128
    d_of = jnp.where(main, row // 64, (q % 8) // 4)
    x_of = jnp.where(main, (row % 64) // 16, q // 8)
    z_of = jnp.where(main, (row // 8) % 2, (q // 2) % 2)
    v_of = jnp.where(main, row % 8, 8 + q % 2)
    target = v_of * 16 + 8 * z_of + 2 * x_of + core
    column = lax.broadcasted_iota(jnp.int32, (160, 160), 1)
    pick_c[...] = (column == target).astype(F32).astype(BF16)
    column = lax.broadcasted_iota(jnp.int32, (160, 320), 1)
    pick[...] = (column == d_of * 160 + target).astype(F32).astype(BF16)
    for ch, (lo, hi, side) in enumerate(SPANS):
        if hi - lo < 2 * side:
            mixed[ch][:, :, side:] = jnp.zeros((4, 8, side), F32)
            parts[ch][:, :, 16:32] = jnp.zeros((4, 2, 16, side), F32)

    stencil = {}
    for xx in range(4):
        for z in range(2):
            r = 8 * z + 2 * xx + core
            base = 2 * z + xx // 2
            late = starts[r] - (4 * band + base - 2)
            w = [lat_w[k, r] for k in range(4)]
            five = [jnp.where(late == 0, w[0], 0.0)]
            five += [jnp.where(late == 0, w[j], w[j - 1]) for j in (1, 2, 3)]
            five += [jnp.where(late == 0, 0.0, w[3])]
            for j in range(5):
                stencil[xx, z, base + j] = five[j]

    spans = [(lo, min(lo + 512, WIDE)) for lo in range(0, WIDE, 512)]
    own_climate.wait()
    own_truth.wait()
    for s in range(2):
        if s == 1:
            other_truth.wait_recv()
        for lo, hi in spans:
            t = jnp.dot(pick[...], tbuf[s, :, lo:hi], preferred_element_type=F32)
            clim = jnp.dot(pick_c[...], cbuf[:, lo:hi], preferred_element_type=F32)
            actual[s, :, lo:hi] = t
            anomaly[s, :, lo:hi] = t - clim

    zmask = (lax.broadcasted_iota(jnp.int32, (8, 384), 0) // 2) % 2 == 0

    def stencil_sum(s, pairs):
        planes = {}
        for pair in pairs:
            both = crs[s, pair].astype(F32)
            planes[2 * pair], planes[2 * pair + 1] = both[0:24], both[24:48]

        def weigh(terms):
            terms = [w * v for w, v in terms]
            return functools.reduce(jnp.add, terms) if terms else None

        result = {}
        for xx in range(4):
            for d in range(2):
                for z in range(2):
                    reach = range(2 * z + xx // 2, 2 * z + xx // 2 + 5)
                    result[d * 64 + xx * 16 + z * 8] = weigh(
                        [(stencil[xx, z, c], planes[c][8 * d : 8 * d + 8]) for c in reach if c in planes]
                    )
            terms = []
            for c in planes:
                w0, w1 = stencil.get((xx, 0, c)), stencil.get((xx, 1, c))
                if w0 is not None or w1 is not None:
                    w = jnp.where(zmask, 0.0 if w0 is None else w0, 0.0 if w1 is None else w1)
                    terms.append((w, planes[c][16:24]))
            result[128 + 8 * xx] = weigh(terms)
        return result

    swap.wait_recv()
    for s in range(2):
        for r, value in stencil_sum(s, (1, 2)).items():
            inner[s, r : r + 8] = value

    @pl.when(not_first)
    def _():
        edges[0].wait_recv()
        edges[2].wait_recv()

    @pl.when(not_last)
    def _():
        edges[1].wait_recv()
        edges[3].wait_recv()

    @pl.when(band == 0)
    def _():
        crs[:, 0] = jnp.zeros((2, 48, 384), BF16)

    @pl.when(band == bands - 1)
    def _():
        crs[:, 3] = jnp.zeros((2, 48, 384), BF16)

    for s in range(2):
        edge = stencil_sum(s, (0, 3))
        for r in range(0, 160, 16):
            rows = []
            for q in (r, r + 8):
                rows.append(inner[s, q : q + 8] if edge[q] is None else inner[s, q : q + 8] + edge[q])
            value = jnp.concatenate(rows, axis=0)
            high = value.astype(BF16)
            fields[0, s, r : r + 16] = high
            fields[1, s, r : r + 16] = (value - high.astype(F32)).astype(BF16)

    going, staying = 1 - half, half

    def coded(block):
        tiles = [block[:, j : j + 128] for j in range(0, block.shape[1], 128)]
        return encode(
            [t[r : r + 8] for r in (0, 16) for t in tiles],
            [t[r : r + 8] for r in (8, 24) for t in tiles],
            [t[32:40] for t in tiles],
        )

    def plain(words):
        n = words.shape[0] // 20
        sqs, ans, tails = decode(words, 2 * n, n)
        rows = [jnp.concatenate(g, axis=1) for g in (sqs[:n], ans[:n], sqs[n:], ans[n:], tails)]
        return jnp.concatenate(rows, axis=0)

    def hand_over(which, rows, ch):
        copies = {}
        messages = [coded(parts[ch][(x + k + 1) % 4, rows]) for k in range(3)]
        for k in range(3):
            xsend[ch][k, which] = messages[k]
        for k in (1, 0, 2):
            copies[k] = send(
                xsend[ch].at[k, which],
                xrecv[ch].at[k, which],
                xssem.at[k, which, ch],
                xrsem.at[k, which, ch],
                across[k],
            )
        return copies

    def collect(which, rows, ch, copies):
        total = parts[ch][x, rows]
        for k in range(3):
            copies[k].wait_recv()
            total += plain(xrecv[ch][k, which])
        return total

    first, second = [], []
    for ch, (lo, hi, side) in enumerate(SPANS):
        width = hi - lo
        even = lax.broadcasted_iota(jnp.int32, (8, side), 0) % 4 < 2
        w = table[:, lo:hi]
        sq = an = None
        for s in range(2):
            fine = jnp.dot(fields[0, s], w, preferred_element_type=F32)
            fine += jnp.dot(fields[1, s], w, preferred_element_type=F32)
            error = fine - actual[s, :, lo:hi]
            true_anomaly = anomaly[s, :, lo:hi]
            e2 = error * error
            ab = (error + true_anomaly) * true_anomaly
            sq = e2 if sq is None else sq + e2
            an = ab if an is None else an + ab
        upper = lax.broadcasted_iota(jnp.int32, (8, width), 0) < 4
        for xx in range(4):
            tail = slice(128 + 8 * xx, 136 + 8 * xx)
            both = [t + pltpu.roll(t, 4, 0) for t in (sq[tail], an[tail])]
            mixed[ch][xx, :, 0:width] = jnp.where(upper, both[0], both[1])
            left, right = mixed[ch][xx, :, 0:side], mixed[ch][xx, :, side:]
            parts[ch][xx, 0, 32:40] = jnp.where(even, left, pltpu.roll(right, 2, 0))
            parts[ch][xx, 1, 32:40] = jnp.where(even, pltpu.roll(left, 6, 0), right)
            for z in range(2):
                r = 16 * xx + 8 * z
                for i, t in enumerate((sq, an)):
                    value = t[r : r + 8] + t[64 + r : 72 + r]
                    parts[ch][xx, z, 8 * i : 8 * i + 8] = value[:, 0:side]
                    parts[ch][xx, z, 16 + 8 * i : 24 + 8 * i, 0 : width - side] = value[:, side:width]
        first.append(hand_over(0, going, ch))

    zcopies = []
    for ch in range(CHUNKS):
        zsend[ch][...] = coded(collect(0, going, ch, first[ch]))
        if ch == 0:
            pl.when(half == 0)(lambda: pl.semaphore_wait(far_in, 1))
        zcopies.append(send(zsend[ch], zrecv[ch], zssem.at[ch], zrsem.at[ch], far))

    for ch in range(CHUNKS):
        second.append(hand_over(1, staying, ch))

    for ch in range(CHUNKS):
        zown[ch][...] = collect(1, staying, ch, second[ch])

    for ch, (start, stop, half_width) in enumerate(SPANS):
        zcopies[ch].wait_recv()
        total = (zown[ch][...] + plain(zrecv[ch][...])) * (1.0 / 32.0)
        for side in range(2):
            lo = start + side * half_width
            hi = min(lo + half_width, stop)
            width = hi - lo
            for which in range(2):
                r = 16 * side + 8 * which
                out[which, 0:8, 0, lo:hi] = total[r : r + 8, 0:width]
                r = 32 + 4 * which + 2 * side
                out[which, 8:10, 0, lo:hi] = total[r : r + 2, 0:width]

    for copy in pending:
        copy.wait_send()

    @pl.when(not_last)
    def _():
        edges[0].wait_send()
        edges[2].wait_send()

    @pl.when(not_first)
    def _():
        edges[1].wait_send()
        edges[3].wait_send()


def per_chunk(buffer):
    return [buffer(side, 20 * (side // 128) + 1) for _, _, side in SPANS]


def shards(model, truth, climate, starts, lat_w, lon_first, lon_w):
    vmem = pl.BlockSpec(memory_space=pltpu.VMEM)
    hbm = pl.BlockSpec(memory_space=pl.ANY)
    maps = pl.pallas_call(
        kernel,
        out_shape=jax.ShapeDtypeStruct((2, 10, 1, WIDE), F32),
        in_specs=[hbm] * 7,
        out_specs=vmem,
        scratch_shapes=[
            pltpu.SMEM((16,), jnp.int32),
            pltpu.SMEM((4, 16), F32),
            pltpu.VMEM((WIDE,), jnp.int32),
            pltpu.VMEM((4, WIDE), BF16),
            pltpu.VMEM((20, 4, COARSE), BF16),
            pltpu.VMEM((2, 320, WIDE), BF16),
            pltpu.VMEM((160, WIDE), BF16),
            pltpu.VMEM((2, 4, 48, 384), BF16),
            pltpu.VMEM((2, 2, 160, 384), BF16),
            pltpu.VMEM((384, WIDE), BF16),
            pltpu.VMEM((160, 320), BF16),
            pltpu.VMEM((160, 160), BF16),
            pltpu.VMEM((2, 160, 384), F32),
            pltpu.VMEM((2, 160, WIDE), F32),
            pltpu.VMEM((2, 160, WIDE), F32),
            per_chunk(lambda side, rows: pltpu.VMEM((4, 8, 2 * side), F32)),
            per_chunk(lambda side, rows: pltpu.VMEM((4, 2, 40, side), F32)),
            per_chunk(lambda side, rows: pltpu.VMEM((3, 2, rows, 128), jnp.int32)),
            per_chunk(lambda side, rows: pltpu.VMEM((3, 2, rows, 128), jnp.int32)),
            per_chunk(lambda side, rows: pltpu.VMEM((rows, 128), jnp.int32)),
            per_chunk(lambda side, rows: pltpu.VMEM((40, side), F32)),
            per_chunk(lambda side, rows: pltpu.VMEM((rows, 128), jnp.int32)),
            pltpu.SemaphoreType.DMA((7,)),
            pltpu.SemaphoreType.DMA((2,)),
            pltpu.SemaphoreType.DMA((5,)),
            pltpu.SemaphoreType.DMA((5,)),
            pltpu.SemaphoreType.DMA((3, 2, CHUNKS)),
            pltpu.SemaphoreType.DMA((3, 2, CHUNKS)),
            pltpu.SemaphoreType.DMA((CHUNKS,)),
            pltpu.SemaphoreType.DMA((CHUNKS,)),
            pltpu.SemaphoreType.REGULAR,
        ],
        compiler_params=pltpu.CompilerParams(
            collective_id=0, has_side_effects=True, vmem_limit_bytes=48 * 2**20
        ),
    )(
        *(
            pltpu.with_memory_space_constraint(operand, pltpu.HBM)
            for operand in (
                model.reshape(20, 4, COARSE),
                truth.reshape(320, WIDE),
                climate.reshape(160, WIDE),
                starts,
                lat_w.T,
                lon_first,
                lon_w,
            )
        )
    )
    return maps[0].reshape(2, 5, 1, WIDE), maps[1].reshape(2, 5, 1, WIDE)


def solution(mesh):
    in_specs = (
        P("date", None, None, "band", None),
        P("date", None, None, "band", None),
        P(None, None, "band", None),
        P("band"),
        P("band", None),
        P(),
        P(),
    )
    out_specs = (P(None, None, ("band", "date"), None), P(None, None, ("band", "date"), None))
    return jax.shard_map(shards, mesh=mesh, in_specs=in_specs, out_specs=out_specs, check_vma=False)
```
